256 devices in a mesh: wide: 32 (over z, x), narrow: 8 (over y, core).
Axes of the slice: x: 4, y: 4, z: 8, core: 2. Of those that a mesh axis runs over, the one named last changes fastest.
Arguments:
- sar_feats: bfloat16 [32768, 1024], P(('wide', 'narrow')), may hold values from -16 to 16
- opt_feats: bfloat16 [32768, 1024], P(('wide', 'narrow')), may hold values from -16 to 16
- w_sar: bfloat16 [1024, 512], replicated, may hold values from -0.0625 to 0.0625
- w_opt: bfloat16 [1024, 512], replicated, may hold values from -0.0625 to 0.0625
- logit_scale: float32 [1], replicated, may hold values from 10 to 100
- partner: int32 [32768], P('wide'), may hold values from 0 to 32767, as said below
Outputs:
- loss: float32 [1], replicated
- grad_sar: bfloat16 [32768, 1024], P(('wide', 'narrow'))
- grad_opt: bfloat16 [32768, 1024], P(('wide', 'narrow'))
- grad_wsar: float32 [1024, 512], P(('wide', 'narrow'))
- grad_wopt: float32 [1024, 512], P(('wide', 'narrow'))
The draws below stay inside these ranges and needn't reach their ends.
Inputs may be any that keep to these rules, and one draw needn't show every extreme that they name: Each optical image is the partner of exactly one radar image.
All inputs are finite; a program needn't handle non-finite values.
Results may differ from the reference program's by a relative error of at most 0.0095.
Values may be sent and summed in bfloat16 or wider, within the bound.
A program may use at most 128 MiB of HBM per device.

```python
import math
import jax
import jax.numpy as jnp
from jax import lax

FEAT = 1024
EMBED = 512
ROWS_DEV = 128
BATCH = 32768


def pairing_order(key):
    return jax.random.permutation(jax.random.fold_in(key, 101), BATCH).astype(jnp.int32)


def spiked(key, values):
    device_count = BATCH // ROWS_DEV
    block_width = FEAT // device_count
    owners = jax.random.permutation(key, device_count).astype(jnp.int32)
    row_block = jnp.arange(BATCH, dtype=jnp.int32) // ROWS_DEV
    col_block = jnp.arange(FEAT, dtype=jnp.int32) // block_width
    spiked_cells = owners[row_block][:, None] == col_block[None, :]
    return jnp.where(spiked_cells, 4.0 * values, values)


def paired_features(key, common, outlier_pull, outlier_keep, align_low, align_high, scale_low, scale_high):
    ordering = pairing_order(key)
    inverse = jnp.zeros((BATCH,), jnp.int32).at[ordering].set(jnp.arange(BATCH, dtype=jnp.int32))
    groups = jax.random.randint(jax.random.fold_in(key, 102), (BATCH,), 0, 64)
    outlier = jax.random.randint(jax.random.fold_in(key, 103), (BATCH,), 0, 64) == 0
    centers = jax.random.normal(jax.random.fold_in(key, 104), (64, FEAT), jnp.float32)
    affinity = jax.random.uniform(jax.random.fold_in(key, 105), (BATCH, 1), jnp.float32, 0.2, 0.8)
    personal = jax.random.normal(jax.random.fold_in(key, 106), (BATCH, FEAT), jnp.float32)
    lifted = jax.random.normal(jax.random.fold_in(key, 107), (1, FEAT), jnp.float32)
    baseline = affinity * centers[groups] + jnp.sqrt(1.0 - affinity * affinity) * personal
    pull_rows = jnp.where(outlier, jnp.float32(-outlier_pull), jnp.float32(common))
    radar = baseline + pull_rows[:, None] * lifted
    alignment = jax.random.uniform(jax.random.fold_in(key, 108), (BATCH, 1), jnp.float32, align_low, align_high)
    alignment = jnp.where(outlier[:, None], jnp.float32(outlier_keep) * alignment, alignment)
    jitter = jax.random.normal(jax.random.fold_in(key, 109), (BATCH, FEAT), jnp.float32)
    blended = alignment * baseline + jnp.sqrt(1.0 - alignment * alignment) * jitter + jnp.float32(common) * lifted
    optical = blended[inverse]
    radar_scale = jnp.exp(jax.random.uniform(jax.random.fold_in(key, 110), (BATCH, 1), jnp.float32, math.log(scale_low), math.log(scale_high)))
    optical_scale = jnp.exp(jax.random.uniform(jax.random.fold_in(key, 111), (BATCH, 1), jnp.float32, math.log(scale_low), math.log(scale_high)))
    radar = spiked(jax.random.fold_in(key, 112), radar * radar_scale)
    optical = spiked(jax.random.fold_in(key, 113), optical * optical_scale)
    return (jnp.clip(radar, -16.0, 16.0), jnp.clip(optical, -16.0, 16.0))


def paired_heads(key):
    leading = jax.random.uniform(jax.random.fold_in(key, 121), (FEAT, EMBED), jnp.float32, -0.0625, 0.0625)
    deviation = jax.random.uniform(jax.random.fold_in(key, 122), (FEAT, EMBED), jnp.float32, -0.0625, 0.0625)
    return (leading, jnp.clip(0.99 * leading + 0.141 * deviation, -0.0625, 0.0625))


def draw_sar_feats(key, part):
    return paired_features(key, 0.3, 0.0, 0.5, 0.3, 0.95, 0.5, 5.0)[0].astype(jnp.bfloat16)


def draw_opt_feats(key, part):
    return paired_features(key, 0.3, 0.0, 0.5, 0.3, 0.95, 0.5, 5.0)[1].astype(jnp.bfloat16)


def draw_w_sar(key, part):
    return paired_heads(key)[0].astype(jnp.bfloat16)


def draw_w_opt(key, part):
    return paired_heads(key)[1].astype(jnp.bfloat16)


def draw_logit_scale(key, part):
    key = jax.random.fold_in(key, 7)
    return jax.random.uniform(key, (1,), jnp.float32, 10.0, 100.0)


def draw_partner(key, part):
    return pairing_order(key)


def setup_inputs(seed: int = 0) -> dict:
    seeds = jax.random.split(jax.random.key(seed), 7)
    sar_feats = draw_sar_feats(jax.random.fold_in(seeds[6], 71), 0)
    opt_feats = draw_opt_feats(jax.random.fold_in(seeds[6], 71), 0)
    w_sar = draw_w_sar(jax.random.fold_in(seeds[6], 71), 0)
    w_opt = draw_w_opt(jax.random.fold_in(seeds[6], 71), 0)
    logit_scale = draw_logit_scale(jax.random.fold_in(seeds[6], 71), 0)
    partner = draw_partner(jax.random.fold_in(seeds[6], 71), 0)
    return dict(sar_feats=sar_feats, opt_feats=opt_feats, w_sar=w_sar, w_opt=w_opt, logit_scale=logit_scale, partner=partner)


def project(features, weight):
    raw = jnp.dot(features, weight, preferred_element_type=jnp.float32)
    inverse = lax.rsqrt(lax.optimization_barrier(jnp.sum(raw * raw, axis=1, keepdims=True)) + 1e-06)
    return (raw, inverse, (raw * inverse).astype(jnp.bfloat16))

def unproject(features, weight, raw, inverse, grad_unit):
    inner = lax.optimization_barrier(jnp.sum(raw * grad_unit, axis=1, keepdims=True))
    grad_raw = (inverse * grad_unit - raw * inverse * inverse * inverse * inner).astype(jnp.bfloat16)
    grad_feat = jnp.dot(grad_raw, weight.T, preferred_element_type=jnp.float32).astype(jnp.bfloat16)
    grad_weight = jnp.dot(features.T, grad_raw, preferred_element_type=jnp.float32)
    return (grad_feat, grad_weight)

def reference(sar_feats, opt_feats, w_sar, w_opt, logit_scale, partner):
    factor = logit_scale[0]
    raw_s, inv_s, unit_s = project(sar_feats, w_sar)
    raw_o, inv_o, unit_o = project(opt_feats, w_opt)
    block = min(512, BATCH)
    count = BATCH // block
    unit_blocks = unit_s.reshape(count, block, EMBED)
    partner_blocks = partner.reshape(count, block)
    columns = jnp.arange(BATCH, dtype=jnp.int32)

    def tile(unit_b, partner_b):
        logits = factor * jnp.dot(unit_b, unit_o.T, preferred_element_type=jnp.float32)
        mask = partner_b[:, None] == columns[None, :]
        return (logits, mask)

    def first(carry, inputs):
        col_max, col_sum, col_pos = carry
        unit_b, partner_b = inputs
        logits, mask = tile(unit_b, partner_b)
        masked = jnp.where(mask, logits, jnp.float32(0.0))
        row_max = lax.optimization_barrier(jnp.max(logits, axis=1, keepdims=True))
        lse_row = row_max[:, 0] + jnp.log(lax.optimization_barrier(jnp.sum(jnp.exp(logits - row_max), axis=1)))
        pos_row = lax.optimization_barrier(jnp.sum(masked, axis=1))
        newmax = jnp.maximum(col_max, lax.optimization_barrier(jnp.max(logits, axis=0)))
        col_sum = col_sum * jnp.exp(col_max - newmax) + lax.optimization_barrier(jnp.sum(jnp.exp(logits - newmax[None, :]), axis=0))
        col_pos = col_pos + lax.optimization_barrier(jnp.sum(masked, axis=0))
        return ((newmax, col_sum, col_pos), (lse_row, pos_row))
    start = (jnp.full((BATCH,), -jnp.inf, jnp.float32), jnp.zeros((BATCH,), jnp.float32), jnp.zeros((BATCH,), jnp.float32))
    (col_max, col_sum, pos_col), (lse_row, pos_row) = lax.scan(first, start, (unit_blocks, partner_blocks))
    lse_col = col_max + jnp.log(col_sum)
    loss = (jnp.sum(lse_row - pos_row) + jnp.sum(lse_col - pos_col)) / (2.0 * BATCH)

    def second(carry, inputs):
        unit_b, partner_b, lse_b = inputs
        logits, mask = tile(unit_b, partner_b)
        gradient = (jnp.exp(logits - lse_b[:, None]) + jnp.exp(logits - lse_col[None, :]) - 2.0 * mask.astype(jnp.float32)) * 0.5
        grad_logits = (factor * gradient).astype(jnp.bfloat16)
        grad_us = jnp.dot(grad_logits, unit_o, preferred_element_type=jnp.float32)
        carry = carry + jnp.dot(grad_logits.T, unit_b, preferred_element_type=jnp.float32)
        return (carry, grad_us)
    grad_uo, grad_us = lax.scan(second, jnp.zeros((BATCH, EMBED), jnp.float32), (unit_blocks, partner_blocks, lse_row))
    grad_us = grad_us.reshape(BATCH, EMBED)
    grad_sar, grad_wsar = unproject(sar_feats, w_sar, raw_s, inv_s, grad_us)
    grad_opt, grad_wopt = unproject(opt_feats, w_opt, raw_o, inv_o, grad_uo)
    return (loss.reshape(1), grad_sar, grad_opt, grad_wsar, grad_wopt)
```

```python
import jax
import jax.numpy as jnp
from jax import lax
from jax.experimental import pallas as pl
from jax.experimental.pallas import tpu as pltpu
from jax.sharding import PartitionSpec as P

NX, NY, NZ = 4, 4, 8
R = 128
E = 512
F = 1024
HALF = 256
TR = NZ * 2 * R
TC = NX * NY * R
LOG2E = 1.4426950408889634
SHIFT = 25.0
MSGS = 240
f32 = jnp.float32
bf16 = jnp.bfloat16
MESH = pl.DeviceIdType.MESH


def dot_nt(a, b):
    return lax.dot_general(a, b, (((1,), (1,)), ((), ())), preferred_element_type=f32)


def dot_nn(a, b):
    return jnp.dot(a, b, preferred_element_type=f32)


def kernel(
    sar_ref, opt_ref, ws_ref, wo_ref, scale_ref, partner_ref,
    loss_ref, gsar_ref, gopt_ref, gws_ref, gwo_ref,
    a_ref, at_ref, b_ref, e_ref, g_ref, raws_ref, rawo_ref,
    part_ref, prow_ref, cid_ref, racc_ref, cacc_ref, pacc_ref,
    rsnd_ref, csnd_ref, rrcv_ref, crcv_ref, rst_ref, cst_ref, rrow_ref,
    acc_ref, gbt_ref, rh0_ref, rh1_ref, th0_ref, th1_ref, p2h0_ref, p2h1_ref,
    qown_ref, qsis_ref, qrcv_ref, qsnd_ref, zp0_ref, zm0_ref, zp_ref, zm_ref,
    fsnd_ref, frcv_ref, ft_ref, gmine_ref, gsnd_ref, grcv_ref, w_ref,
    sx_ref, sy_ref, rx_ref, ry_ref, sx2_ref, sy2_ref, rx2_ref, ry2_ref,
    u_ref, rz_ref, fin_ref, sis_ref, lr_ref,
    ssem, rsem,
):
    wide = lax.axis_index("wide")
    narrow = lax.axis_index("narrow")
    x, y, z, c = lax.rem(wide, NX), narrow // 2, wide // NX, lax.rem(narrow, 2)

    def dev(dx=0, dy=0, dz=0, dc=0):
        px = lax.rem(x + (dx % NX), NX)
        py = lax.rem(y + (dy % NY), NY)
        pz = lax.rem(z + (dz % NZ), NZ)
        pc = lax.rem(c + (dc % 2), 2)
        return (pz * NX + px, py * 2 + pc)

    plane = [(i, j) for i in range(NX) for j in range(NY) if (i, j) != (0, 0)]
    zcs = [(i, j) for i in range(NZ) for j in range(2) if (i, j) != (0, 0)]

    barrier = pltpu.get_barrier_semaphore()
    for i, j in plane:
        pl.semaphore_signal(barrier, inc=1, device_id=dev(dx=i, dy=j), device_id_type=MESH)
    for i, j in zcs:
        pl.semaphore_signal(barrier, inc=1, device_id=dev(dz=i, dc=j), device_id_type=MESH)

    sent = []

    def send(src, dst, device):
        m = len(sent)
        copy = pltpu.make_async_remote_copy(
            src_ref=src, dst_ref=dst, send_sem=ssem.at[m], recv_sem=rsem.at[m],
            device_id=device, device_id_type=MESH,
        )
        copy.start()
        sent.append(copy)
        return copy

    def brow(dx, dy):
        return ((dx % NX) * NY + (dy % NY)) * R

    def arow(dz, dc):
        return ((dz % NZ) * 2 + dc % 2) * R

    scale = scale_ref[0]

    def project(feat_ref, w_ref, raw_ref, dst_ref):
        raw = dot_nn(feat_ref[...], w_ref[...])
        inv = lax.rsqrt(jnp.sum(raw * raw, axis=1, keepdims=True) + 1e-06)
        raw_ref[...] = raw
        dst_ref[pl.ds(0, R), :] = (raw * inv).astype(bf16)
        return inv

    inv_o = project(opt_ref, wo_ref, rawo_ref, b_ref)
    inv_s = project(sar_ref, ws_ref, raws_ref, a_ref)
    own_partner = partner_ref[pl.ds(narrow, 1), :].astype(f32)
    part_ref[0] = jnp.broadcast_to(own_partner, (8, R))
    core0 = c == 0
    sar = sar_ref[...]
    opt = opt_ref[...]
    fsnd_ref[...] = jnp.where(core0, opt, sar)

    pl.semaphore_wait(barrier, len(plane) + len(zcs))

    bx, by, az = {}, {}, {}
    own_b = b_ref.at[pl.ds(0, R)]
    own_a = a_ref.at[pl.ds(0, R)]
    up = send(own_a, a_ref.at[pl.ds(arow(-1, 0), R)], dev(dz=1))
    down = send(own_a, a_ref.at[pl.ds(arow(1, 0), R)], dev(dz=-1))
    for d in (1, 3, 2):
        bx[d] = send(own_b, b_ref.at[pl.ds(brow(-d, 0), R)], dev(dx=d))
        by[d] = send(own_b, b_ref.at[pl.ds(brow(0, -d), R)], dev(dy=d))
    sister = [send(own_a, a_ref.at[pl.ds(arow(0, 1), R)], dev(dc=1))]
    parts = [
        send(part_ref.at[0], part_ref.at[((-i) % NZ) * 2 + j], dev(dz=i, dc=j)) for i, j in zcs
    ]
    fcopy = send(fsnd_ref, frcv_ref, dev(dc=1))

    ft_ref[:, pl.ds(0, R)] = jnp.where(core0, sar, opt).T
    lane = lax.broadcasted_iota(jnp.int32, (8, R), 1)
    for i in range(NX):
        for j in range(NY):
            wx = z * NX + lax.rem(x + i, NX)
            ny = lax.rem(y + j, NY) * 2 + c
            base = (wx * (NY * 2) + ny) * R
            cid_ref[:, pl.ds(brow(i, j), R)] = (lane + base).astype(f32)

    def transpose_a(row):
        at_ref[:, pl.ds(row, R)] = a_ref[pl.ds(row, R), :].T

    transpose_a(0)

    late = []
    for d in (1, 3, 2):
        bx[d].wait_recv()
        blk = b_ref.at[pl.ds(brow(-d, 0), R), pl.ds(0, HALF)]
        for dy in (1, 3, 2):
            late.append(send(
                blk, b_ref.at[pl.ds(brow(-d, -dy), R), pl.ds(0, HALF)], dev(dy=dy)))
        by[d].wait_recv()
        blk = b_ref.at[pl.ds(brow(0, -d), R), pl.ds(HALF, HALF)]
        for dx in (1, 3, 2):
            late.append(send(
                blk, b_ref.at[pl.ds(brow(-dx, -d), R), pl.ds(HALF, HALF)], dev(dx=dx)))
        up.wait_recv()
        blk = a_ref.at[pl.ds(arow(-len(sister), 0), R)]
        down.wait_recv()
        blk2 = a_ref.at[pl.ds(arow(len(sister), 0), R)]
        s = len(sister)
        if s < 3:
            up = send(blk, a_ref.at[pl.ds(arow(-s - 1, 0), R)], dev(dz=1))
            down = send(blk2, a_ref.at[pl.ds(arow(s + 1, 0), R)], dev(dz=-1))
        else:
            up = send(
                blk.at[:, pl.ds(0, HALF)],
                a_ref.at[pl.ds(arow(4, 0), R), pl.ds(0, HALF)], dev(dz=1))
            down = send(
                blk2.at[:, pl.ds(HALF, HALF)],
                a_ref.at[pl.ds(arow(4, 0), R), pl.ds(HALF, HALF)], dev(dz=-1))
        late.append(send(blk, a_ref.at[pl.ds(arow(-s, 1), R)], dev(dc=1)))
        late.append(send(blk2, a_ref.at[pl.ds(arow(s, 1), R)], dev(dc=1)))
        sister.append(None)
        transpose_a(arow(-s, 0))
        transpose_a(arow(s, 0))
    up.wait_recv()
    down.wait_recv()
    late.append(send(
        a_ref.at[pl.ds(arow(4, 0), R)], a_ref.at[pl.ds(arow(4, 1), R)], dev(dc=1)))
    transpose_a(arow(4, 0))
    for copy in parts:
        copy.wait_recv()
    for q in range(NZ * 2):
        prow_ref[pl.ds(q * R, R), :] = jnp.broadcast_to(part_ref[q][0:1, :], (R, R)).T
    fcopy.wait_recv()
    ft_ref[:, pl.ds(R, R)] = frcv_ref[...].T
    sister[0].wait_recv()
    for copy in late:
        copy.wait_recv()
    for d in range(NZ):
        transpose_a(arow(d, 1))

    mul = scale * (0.5 * LOG2E)
    up_factor = 5.184705528587072e21
    cacc_ref[...] = jnp.zeros_like(cacc_ref)
    CH = 32

    @pl.loop(0, NZ)
    def _(rb):
        r0 = pl.multiple_of(rb * HALF, HALF)
        a_blk = a_ref[pl.ds(r0, HALF), :]
        for sl in range(NX):
            e_ref[sl, pl.ds(r0, HALF), :] = dot_nt(a_blk, b_ref[pl.ds(sl * E, E), :])
        for sl in range(NX):
            c1 = jnp.zeros((8, E), f32)
            c2 = jnp.zeros((8, E), f32)
            for ch in range(HALF // CH):
                rows = pl.ds(pl.multiple_of(r0 + ch * CH, CH), CH)
                e = jnp.exp2(e_ref[sl, rows, :] * mul - SHIFT * LOG2E)
                e_ref[sl, rows, :] = e
                q1 = e * e
                u = e * up_factor
                q2 = u * u
                c1 = c1 + jnp.sum(q1.reshape(CH // 8, 8, E), axis=0)
                c2 = c2 + jnp.sum(q2.reshape(CH // 8, 8, E), axis=0)
                r1 = (q1[:, 0:128] + q1[:, 128:256]) + (q1[:, 256:384] + q1[:, 384:512])
                r2 = (q2[:, 0:128] + q2[:, 128:256]) + (q2[:, 256:384] + q2[:, 384:512])
                if sl > 0:
                    r1 = r1 + racc_ref[0, rows, :]
                    r2 = r2 + racc_ref[1, rows, :]
                racc_ref[0, rows, :] = r1
                racc_ref[1, rows, :] = r2
            cols = pl.ds(sl * E, E)
            cacc_ref[0, :, cols] += c1
            cacc_ref[1, :, cols] += c2

    ones = jnp.full((8, R), 0.125, bf16)
    rmsg, cmsg = [], []
    for i, j in [(0, 0)] + zcs:
        q = i * 2 + j
        for k in range(2):
            v = racc_ref[k, pl.ds(q * R, R), :]
            hi = v.astype(bf16)
            lo = (v - hi.astype(f32)).astype(bf16)
            rsnd_ref[q, pl.ds(8 * k, 8), :] = dot_nt(ones, hi) + dot_nt(ones, lo)
        if q:
            rmsg.append(send(rsnd_ref.at[q], rrcv_ref.at[q], dev(dz=i, dc=j)))
    for i, j in [(0, 0)] + plane:
        p = i * NY + j
        for k in range(2):
            csnd_ref[p, pl.ds(8 * k, 8), :] = cacc_ref[k, :, pl.ds(p * R, R)]
        if p:
            cmsg.append(send(csnd_ref.at[p], crcv_ref.at[p], dev(dx=i, dy=j)))

    half_scale = scale * 0.5

    def finish(total):
        s1 = jnp.sum(total[0:8], axis=0, keepdims=True)
        s2 = jnp.sum(total[8:16], axis=0, keepdims=True)
        lse = jnp.where(
            s1 > 1.9287498e-22, jnp.log(s1) + 2.0 * SHIFT, jnp.log(s2) - 2.0 * SHIFT)
        factor = jnp.exp(SHIFT - 0.5 * lse) * jnp.sqrt(jnp.full((1, R), half_scale, f32))
        return lse, jnp.broadcast_to(factor, (8, R))

    total = rsnd_ref[0]
    for n, copy in enumerate(rmsg):
        copy.wait_recv()
        total = total + rrcv_ref[n + 1]
    lse_row, factor = finish(total)
    rst_ref[0] = factor
    rmsg = [
        send(rst_ref.at[0], rst_ref.at[((-i) % NZ) * 2 + j], dev(dz=i, dc=j)) for i, j in zcs
    ]
    total = csnd_ref[0]
    for n, copy in enumerate(cmsg):
        copy.wait_recv()
        total = total + crcv_ref[n + 1]
    lse_col, factor = finish(total)
    cst_ref[:, pl.ds(0, R)] = factor
    cmsg = [
        send(cst_ref.at[:, pl.ds(0, R)], cst_ref.at[:, pl.ds(brow(-i, -j), R)], dev(dx=i, dy=j))
        for i, j in plane
    ]
    rrow_ref[pl.ds(0, R), :] = jnp.broadcast_to(rst_ref[0][0:1, :], (R, R)).T
    for (i, j), copy in zip(zcs, rmsg):
        copy.wait_recv()
        q = ((-i) % NZ) * 2 + j
        rrow_ref[pl.ds(q * R, R), :] = jnp.broadcast_to(rst_ref[q][0:1, :], (R, R)).T
    for copy in cmsg:
        copy.wait_recv()

    h0, h1 = {}, {}
    for n, sl in enumerate((2, 1, 3, 0)):
        acc_ref[...] = jnp.zeros_like(acc_ref)

        @pl.loop(0, NZ)
        def _(rb):
            r0 = pl.multiple_of(rb * HALF, HALF)
            for ch in range(HALF // CH):
                rows = pl.ds(pl.multiple_of(r0 + ch * CH, CH), CH)
                rr = rrow_ref[rows, :].reshape(CH // 8, 8, R)
                pr = prow_ref[rows, :].reshape(CH // 8, 8, R)
                pos = None
                for lg in range(NY):
                    lanes = pl.ds(lg * R, R)
                    e = e_ref[sl, rows, lanes].reshape(CH // 8, 8, R)
                    cols = pl.ds(sl * E + lg * R, R)
                    u = e * rr
                    v = e * cst_ref[:, cols][None]
                    hit = pr == cid_ref[:, cols][None]
                    g = u * u + v * v - jnp.where(hit, scale, 0.0)
                    pe = jnp.where(hit, e, 0.0)
                    pos = pe if pos is None else pos + pe
                    g_ref[sl, rows, lanes] = g.reshape(CH, R).astype(bf16)
                pos = pos.reshape(CH, R)
                if n > 0:
                    pos = pos + pacc_ref[rows, :]
                pacc_ref[rows, :] = pos
            acc_ref[...] += dot_nn(
                at_ref[:, pl.ds(r0, HALF)], g_ref[sl, pl.ds(r0, HALF), :])

        gbt_ref[sl] = acc_ref[...].astype(bf16)
        if sl:
            h0[sl] = send(gbt_ref.at[sl, pl.ds(0, HALF)], rh0_ref.at[sl - 1], dev(dx=sl))
        for dy in (2, 1, 3):
            h1[sl, dy] = send(
                gbt_ref.at[sl, pl.ds(HALF, HALF), pl.ds(dy * R, R)],
                rh1_ref.at[dy - 1, sl], dev(dy=dy))

    qmsg = {}

    def radar(d):
        total = None
        for sl in range(NX):
            t = dot_nn(g_ref[sl, pl.ds(arow(d, 0), HALF), :], b_ref[pl.ds(sl * E, E), :])
            total = t if total is None else total + t
        qown_ref[d % NZ] = total[0:R]
        qsis_ref[d % NZ] = total[R:].astype(bf16)
        qmsg[d] = send(qsis_ref.at[d % NZ], qrcv_ref.at[d % NZ], dev(dc=1))

    def chip_sum(d):
        qmsg[d].wait_recv()
        return qown_ref[d % NZ] + qrcv_ref[d % NZ].astype(f32)

    def ring(d, sign, prev):
        q = chip_sum(d)
        k = abs(d)
        if k == 3:
            prev.wait_recv()
            if sign > 0:
                left = q[:, :HALF] + zp0_ref[...].astype(f32)
                qsnd_ref[d % NZ, :, pl.ds(0, HALF)] = left.astype(bf16)
                qsnd_ref[d % NZ, :, pl.ds(HALF, HALF)] = q[:, HALF:].astype(bf16)
            else:
                right = q[:, HALF:] + zm0_ref[...].astype(f32)
                qsnd_ref[d % NZ, :, pl.ds(0, HALF)] = q[:, :HALF].astype(bf16)
                qsnd_ref[d % NZ, :, pl.ds(HALF, HALF)] = right.astype(bf16)
        else:
            prev.wait_recv()
            inc = zp_ref if sign > 0 else zm_ref
            qsnd_ref[d % NZ] = (q + inc[2 - k].astype(f32)).astype(bf16)
        dst = zp_ref if sign > 0 else zm_ref
        return send(qsnd_ref.at[d % NZ], dst.at[3 - k], dev(dz=sign))

    radar(4)
    radar(3)
    qsnd_ref[4] = chip_sum(4).astype(bf16)
    zp = send(qsnd_ref.at[4, :, pl.ds(0, HALF)], zp0_ref, dev(dz=1))
    zm = send(qsnd_ref.at[4, :, pl.ds(HALF, HALF)], zm0_ref, dev(dz=-1))
    radar(-3)
    radar(2)
    radar(-2)
    zp = ring(3, 1, zp)
    zm = ring(-3, -1, zm)
    radar(1)
    radar(-1)
    radar(0)

    pos = pacc_ref[...]
    pos = jnp.where(pos > 0.0, 2.0 * (jnp.log(jnp.where(pos > 0.0, pos, 1.0)) + SHIFT), 0.0)
    pos = jnp.sum(pos.reshape(TR // 8, 8, R), axis=0)
    row0 = lax.broadcasted_iota(jnp.int32, (8, R), 0) == 0
    both = jnp.broadcast_to(lse_row + lse_col, (8, R))
    lr_ref[0] = jnp.where(row0, both, 0.0) - 2.0 * pos
    lmsg = [send(lr_ref.at[0], lr_ref.at[NX - d], dev(dx=d)) for d in range(1, NX)]

    zp = ring(2, 1, zp)
    zm = ring(-2, -1, zm)

    t0 = gbt_ref[0, pl.ds(0, HALF), :].astype(f32)
    for d in (2, 1, 3):
        h0[d].wait_recv()
        t0 = t0 + rh0_ref[d - 1].astype(f32)
    th0_ref[...] = t0.astype(bf16)
    p2a = [
        send(th0_ref.at[:, pl.ds(d * R, R)], p2h0_ref.at[d - 1], dev(dy=d)) for d in range(1, NY)
    ]
    gh0 = t0[:, :R]
    p2b = []
    for sl in (2, 1, 3, 0):
        t1 = gbt_ref[sl, pl.ds(HALF, HALF), pl.ds(0, R)].astype(f32)
        for d in (2, 1, 3):
            h1[sl, d].wait_recv()
            t1 = t1 + rh1_ref[d - 1, sl].astype(f32)
        if sl:
            th1_ref[sl] = t1.astype(bf16)
            p2b.append(send(th1_ref.at[sl], p2h1_ref.at[sl - 1], dev(dx=sl)))
        else:
            gh1 = t1

    def gather_loss(first, n, me, msgs):
        for copy in msgs:
            copy.wait_recv()
        t = jnp.zeros((8, R), f32)
        for i in range(n):
            t = t + lr_ref[first + lax.rem(i - me + n, n)]
        return t

    lr_ref[4] = gather_loss(0, NX, x, lmsg)
    lmsg = [send(lr_ref.at[4], lr_ref.at[4 + NY - d], dev(dy=d)) for d in range(1, NY)]

    zp = ring(1, 1, zp)
    zm = ring(-1, -1, zm)

    def unproject(grad_unit, raw_ref, inv):
        raw = raw_ref[...]
        inner = jnp.sum(raw * grad_unit, axis=1, keepdims=True)
        return (inv * grad_unit - raw * (inv * inv * inv * inner)).astype(bf16)

    for copy in p2a:
        copy.wait_recv()
    for copy in p2b:
        copy.wait_recv()
    for d in range(NX - 1):
        gh0 = gh0 + p2h0_ref[d].astype(f32)
        gh1 = gh1 + p2h1_ref[d].astype(f32)
    grad_uo = jnp.concatenate([gh0.T, gh1.T], axis=1)
    gro = unproject(grad_uo, rawo_ref, inv_o)

    q0 = chip_sum(0)
    zp.wait_recv()
    zm.wait_recv()
    grad_us = q0 + zp_ref[2].astype(f32) + zm_ref[2].astype(f32)
    grs = unproject(grad_us, raws_ref, inv_s)

    gsnd_ref[...] = jnp.where(core0, gro, grs)
    gcopy = send(gsnd_ref, grcv_ref, dev(dc=1))
    gmine_ref[...] = jnp.where(core0, grs, gro)
    gopt_ref[...] = dot_nt(gro, wo_ref[...]).astype(bf16)
    lr_ref[8] = gather_loss(4, NY, y, lmsg)
    lmsg = [send(lr_ref.at[8], lr_ref.at[8 + NZ - d], dev(dz=d)) for d in range(1, NZ)]
    gcopy.wait_recv()

    w_ref[...] = dot_nn(ft_ref[:, pl.ds(0, R)], gmine_ref[...]) + dot_nn(
        ft_ref[:, pl.ds(R, R)], grcv_ref[...])
    for ix in range(NX):
        for iy in range(NY):
            for zz in range(0, NZ, 2):
                lo = ((zz * NX + ix) * NY + iy) * 8
                hi = (((zz + 1) * NX + ix) * NY + iy) * 8
                left = jnp.concatenate(
                    [w_ref[pl.ds(lo, 8), pl.ds(0, HALF)], w_ref[pl.ds(hi, 8), pl.ds(0, HALF)]], 0)
                right = jnp.concatenate(
                    [w_ref[pl.ds(lo, 8), pl.ds(HALF, HALF)],
                     w_ref[pl.ds(hi, 8), pl.ds(HALF, HALF)]], 0)
                sx_ref[ix, pl.ds(iy * 64 + zz * 8, 16), :] = left.astype(bf16)
                sy_ref[iy, pl.ds(ix * 64 + zz * 8, 16), :] = right.astype(bf16)
    wx, wy = {}, {}
    for d in (2, 1, 3):
        wx[d] = send(sx_ref.at[lax.rem(x + d, NX)], rx_ref.at[d - 1], dev(dx=d))
        wy[d] = send(sy_ref.at[lax.rem(y + d, NY)], ry_ref.at[d - 1], dev(dy=d))
    gsar_ref[...] = dot_nt(grs, ws_ref[...]).astype(bf16)
    tx = sx_ref[x].astype(f32)
    ty = sy_ref[y].astype(f32)
    for d in (1, 3, 2):
        wx[d].wait_recv()
        tx = tx + rx_ref[d - 1].astype(f32)
        wy[d].wait_recv()
        ty = ty + ry_ref[d - 1].astype(f32)
    sx2_ref[...] = tx.astype(bf16).reshape(NY, 64, HALF)
    sy2_ref[...] = ty.astype(bf16).reshape(NX, 64, HALF)
    for d in (2, 1, 3):
        wx[d] = send(sx2_ref.at[lax.rem(y + d, NY)], rx2_ref.at[d - 1], dev(dy=d))
        wy[d] = send(sy2_ref.at[lax.rem(x + d, NX)], ry2_ref.at[d - 1], dev(dx=d))
    lr_ref[16] = gather_loss(8, NZ, z, lmsg)
    lmsg = [send(lr_ref.at[16], lr_ref.at[17], dev(dc=1))]
    tx = sx2_ref[y].astype(f32)
    ty = sy2_ref[x].astype(f32)
    for d in (1, 3, 2):
        wx[d].wait_recv()
        tx = tx + rx2_ref[d - 1].astype(f32)
        wy[d].wait_recv()
        ty = ty + ry2_ref[d - 1].astype(f32)
    u_ref[:, :, pl.ds(0, HALF)] = tx.reshape(NZ, 8, HALF)
    u_ref[:, :, pl.ds(HALF, HALF)] = ty.reshape(NZ, 8, HALF)
    wz = [
        send(u_ref.at[lax.rem(z + d, NZ)], rz_ref.at[d - 1], dev(dz=d)) for d in range(1, NZ)
    ]
    loss_ref[0] = jnp.sum(gather_loss(16, 2, c, lmsg)) * (1.0 / (2.0 * NX * NY * NZ * 2 * R))
    total = u_ref[z]
    for d in range(1, NZ):
        wz[d - 1].wait_recv()
        total = total + rz_ref[d - 1]
    fin_ref[...] = total
    last = send(fin_ref, sis_ref, dev(dc=1))
    last.wait_recv()
    other = sis_ref[...]
    s_sum = jnp.where(core0, total, other)
    o_sum = jnp.where(core0, other, total)
    gws_ref[...] = jnp.where(core0, s_sum[0:4], s_sum[4:8])
    gwo_ref[...] = jnp.where(core0, o_sum[0:4], o_sum[4:8])

    for copy in sent:
        copy.wait_send()


def local(sar_feats, opt_feats, w_sar, w_opt, logit_scale, partner):
    V = pltpu.VMEM
    scratch = [
        V((TR, E), bf16), V((E, TR), bf16), V((TC, E), bf16),
        V((NX, TR, E), f32), V((NX, TR, E), bf16), V((R, E), f32), V((R, E), f32),
        V((16, 8, R), f32), V((TR, R), f32), V((8, TC), f32),
        V((2, TR, R), f32), V((2, 8, TC), f32), V((TR, R), f32),
        V((16, 16, R), f32), V((16, 16, R), f32), V((16, 16, R), f32), V((16, 16, R), f32),
        V((16, 8, R), f32), V((8, TC), f32), V((TR, R), f32),
        V((E, E), f32), V((NX, E, E), bf16), V((3, HALF, E), bf16), V((3, NX, HALF, R), bf16),
        V((HALF, E), bf16), V((NX, HALF, R), bf16), V((3, HALF, R), bf16), V((3, HALF, R), bf16),
        V((NZ, R, E), f32), V((NZ, R, E), bf16), V((NZ, R, E), bf16), V((NZ, R, E), bf16),
        V((R, HALF), bf16), V((R, HALF), bf16), V((3, R, E), bf16), V((3, R, E), bf16),
        V((R, F), bf16), V((R, F), bf16), V((F, 2 * R), bf16),
        V((R, E), bf16), V((R, E), bf16), V((R, E), bf16), V((F, E), f32),
        V((NX, HALF, HALF), bf16), V((NY, HALF, HALF), bf16),
        V((3, HALF, HALF), bf16), V((3, HALF, HALF), bf16),
        V((NY, 64, HALF), bf16), V((NX, 64, HALF), bf16),
        V((3, 64, HALF), bf16), V((3, 64, HALF), bf16),
        V((NZ, 8, E), f32), V((NZ - 1, 8, E), f32), V((8, E), f32), V((8, E), f32),
        V((18, 8, R), f32),
        pltpu.SemaphoreType.DMA((MSGS,)), pltpu.SemaphoreType.DMA((MSGS,)),
    ]
    vm = pl.BlockSpec(memory_space=pltpu.VMEM)
    sm = pl.BlockSpec(memory_space=pltpu.SMEM)
    return pl.pallas_call(
        kernel,
        out_shape=(
            jax.ShapeDtypeStruct((1,), f32),
            jax.ShapeDtypeStruct((R, F), bf16),
            jax.ShapeDtypeStruct((R, F), bf16),
            jax.ShapeDtypeStruct((4, E), f32),
            jax.ShapeDtypeStruct((4, E), f32),
        ),
        in_specs=[vm, vm, vm, vm, sm, vm],
        out_specs=(sm, vm, vm, vm, vm),
        scratch_shapes=scratch,
        compiler_params=pltpu.CompilerParams(
            collective_id=0, has_side_effects=True, vmem_limit_bytes=62 * 1024 * 1024),
        name="contrastive",
    )(sar_feats, opt_feats, w_sar, w_opt, logit_scale, partner.reshape(NY * 2, R))


def solution(mesh):
    return jax.shard_map(
        local,
        mesh=mesh,
        in_specs=(
            P(("wide", "narrow"), None),
            P(("wide", "narrow"), None),
            P(),
            P(),
            P(),
            P("wide"),
        ),
        out_specs=(
            P(),
            P(("wide", "narrow"), None),
            P(("wide", "narrow"), None),
            P(("wide", "narrow"), None),
            P(("wide", "narrow"), None),
        ),
        check_vma=False,
    )
```

```python
import jax
import jax.numpy as jnp
from jax import lax
from jax.experimental import pallas as pl
from jax.experimental.pallas import tpu as pltpu
from jax.sharding import PartitionSpec as P

NX, NY, NZ = 4, 4, 8
R = 128
E = 512
F = 1024
HALF = 256
TR = NZ * 2 * R
TC = NX * NY * R
LOG2E = 1.4426950408889634
SHIFT = 25.0
UP = 5.184705528587072e21
DOWN = 1.9287498e-22
MSGS = 256
ORDER = (0, 1, 7, 2, 6, 3, 5, 4)
NEAR = 5 * 2 * R
f32 = jnp.float32
bf16 = jnp.bfloat16
MESH = pl.DeviceIdType.MESH


def dot_nt(a, b):
    return lax.dot_general(a, b, (((1,), (1,)), ((), ())), preferred_element_type=f32)


def dot_nn(a, b):
    return jnp.dot(a, b, preferred_element_type=f32)


def kernel(
    sar_ref, opt_ref, ws_ref, wo_ref, scale_ref, partner_ref,
    loss_ref, gsar_ref, gopt_ref, gws_ref, gwo_ref,
    a_ref, at_ref, b_ref, e_ref, g_ref, raws_ref, rawo_ref,
    part_ref, prow_ref, cid_ref, racc_ref, cacc_ref, pacc_ref,
    rsnd_ref, csnd_ref, rrcv_ref, crcv_ref, lses_ref, cfac_ref, rfac_ref, rhalf_ref,
    cst_ref, rrow_ref, gbt_ref, rh0_ref, rh1_ref, th0_ref, th1_ref, p2h0_ref, p2h1_ref,
    qown_ref, qsis_ref, qrcv_ref, qsnd_ref, zp_ref, zm_ref,
    frcv_ref, ft_ref, gmine_ref, gsnd_ref, grcv_ref,
    sx_ref, sy_ref, rx_ref, ry_ref, sx2_ref, sy2_ref, rx2_ref, ry2_ref,
    u_ref, rz_ref, fin_ref, sis_ref, lr_ref,
    ssem, rsem,
):
    wide = lax.axis_index("wide")
    narrow = lax.axis_index("narrow")
    x, y, z, c = lax.rem(wide, NX), narrow // 2, wide // NX, lax.rem(narrow, 2)

    def dev(dx=0, dy=0, dz=0, dc=0):
        px = lax.rem(x + (dx % NX), NX)
        py = lax.rem(y + (dy % NY), NY)
        pz = lax.rem(z + (dz % NZ), NZ)
        pc = lax.rem(c + (dc % 2), 2)
        return (pz * NX + px, py * 2 + pc)

    plane = [(i, j) for i in range(NX) for j in range(NY) if (i, j) != (0, 0)]

    barrier = pltpu.get_barrier_semaphore()
    for i, j in plane:
        pl.semaphore_signal(barrier, inc=1, device_id=dev(dx=i, dy=j), device_id_type=MESH)
    for i in range(1, NZ):
        pl.semaphore_signal(barrier, inc=1, device_id=dev(dz=i), device_id_type=MESH)
    pl.semaphore_signal(barrier, inc=1, device_id=dev(dc=1), device_id_type=MESH)

    sent = []

    def send(src, dst, device):
        m = len(sent)
        copy = pltpu.make_async_remote_copy(
            src_ref=src, dst_ref=dst, send_sem=ssem.at[m], recv_sem=rsem.at[m],
            device_id=device, device_id_type=MESH,
        )
        copy.start()
        sent.append(copy)
        return copy

    def brow(dx, dy):
        return ((dx % NX) * NY + (dy % NY)) * R

    def arow(dz, dc):
        return (ORDER.index(dz % NZ) * 2 + dc % 2) * R

    scale = scale_ref[0]

    def project(feat_ref, w_ref, raw_ref, dst_ref):
        raw = dot_nn(feat_ref[...], w_ref[...])
        inv = lax.rsqrt(jnp.sum(raw * raw, axis=1, keepdims=True) + 1e-06)
        raw_ref[...] = raw
        dst_ref[pl.ds(0, R), :] = (raw * inv).astype(bf16)
        return inv

    inv_o = project(opt_ref, wo_ref, rawo_ref, b_ref)
    inv_s = project(sar_ref, ws_ref, raws_ref, a_ref)
    own_partner = partner_ref[pl.ds(narrow, 1), :].astype(f32)
    part_ref[0, 0] = jnp.broadcast_to(own_partner, (8, R))
    core0 = c == 0

    pl.semaphore_wait(barrier, len(plane) + NZ)

    bx, by, late, sis = {}, {}, {}, {}
    own_b = b_ref.at[pl.ds(0, R)]
    lanes = [pl.ds(0, HALF), pl.ds(HALF, HALF)]

    def zsend(h, src, dst, sign):
        return send(
            a_ref.at[pl.ds(arow(src, 0), R), lanes[h]],
            a_ref.at[pl.ds(arow(dst, 0), R), lanes[h]], dev(dz=sign))

    up = [zsend(h, 0, -1, 1) for h in range(2)]
    down = [zsend(h, 0, 1, -1) for h in range(2)]
    for d in (1, 3, 2):
        bx[d] = send(own_b, b_ref.at[pl.ds(brow(-d, 0), R)], dev(dx=d))
        by[d] = send(own_b, b_ref.at[pl.ds(brow(0, -d), R)], dev(dy=d))

    def to_sister(d):
        sis[d % NZ] = send(
            a_ref.at[pl.ds(arow(d, 0), R)], a_ref.at[pl.ds(arow(d, 1), R)], dev(dc=1))

    to_sister(0)
    parts = [
        send(part_ref.at[0, 0], part_ref.at[0, (-i) % NZ], dev(dz=i)) for i in range(1, NZ)
    ]
    sar = sar_ref[...]
    opt = opt_ref[...]
    fcopy = [
        send(sar_ref, frcv_ref.at[0], dev(dc=1)), send(opt_ref, frcv_ref.at[1], dev(dc=1))
    ]
    lane = lax.broadcasted_iota(jnp.int32, (8, R), 1)
    for i in range(NX):
        for j in range(NY):
            wx = z * NX + lax.rem(x + i, NX)
            ny = lax.rem(y + j, NY) * 2 + c
            base = (wx * (NY * 2) + ny) * R
            cid_ref[:, pl.ds(brow(i, j), R)] = (lane + base).astype(f32)

    def transpose_a(row):
        at_ref[:, pl.ds(row, R)] = a_ref[pl.ds(row, R), :].T

    def ring_step(k):
        for h in range(2):
            up[h].wait_recv()
            if k < 3 or h == 0:
                up[h] = zsend(h, -k, -k - 1, 1)
            down[h].wait_recv()
            if k < 3 or h == 1:
                down[h] = zsend(h, k, k + 1, -1)
        to_sister(-k)
        to_sister(k)

    def plane_step(d):
        bx[d].wait_recv()
        for dy in (1, 3, 2):
            late[(-d) % NX, (-dy) % NY, 0] = send(
                b_ref.at[pl.ds(brow(-d, 0), R), lanes[0]],
                b_ref.at[pl.ds(brow(-d, -dy), R), lanes[0]], dev(dy=dy))
        by[d].wait_recv()
        for dx in (1, 3, 2):
            late[(-dx) % NX, (-d) % NY, 1] = send(
                b_ref.at[pl.ds(brow(0, -d), R), lanes[1]],
                b_ref.at[pl.ds(brow(-dx, -d), R), lanes[1]], dev(dx=dx))

    ring_step(1)
    plane_step(1)
    plane_step(3)
    for k in (0, 1, -1):
        transpose_a(arow(k, 0))
    ft_ref[0, :, pl.ds(0, R)] = sar.T
    ft_ref[1, :, pl.ds(0, R)] = opt.T
    plane_step(2)
    ring_step(2)
    for k in (2, -2):
        transpose_a(arow(k, 0))
    for t in range(2):
        fcopy[t].wait_recv()
        ft_ref[t, :, pl.ds(R, R)] = frcv_ref[t].T
    for copy in parts:
        copy.wait_recv()
    pcopy = send(part_ref.at[0], part_ref.at[1], dev(dc=1))
    for k in (0, 1, -1):
        sis[k % NZ].wait_recv()
        transpose_a(arow(k, 1))
    mul = scale * (0.5 * LOG2E)
    CH = 64

    def logits(sl, lo, hi):
        for i, j, h in sorted(late):
            if i == sl and lo == 0:
                late[i, j, h].wait_recv()
        e_ref[sl, pl.ds(lo, hi - lo), :] = dot_nt(
            a_ref[pl.ds(lo, hi - lo), :], b_ref[pl.ds(sl * E, E), :])

    def exponentials(sl, lo, hi, first):
        c1 = jnp.zeros((8, E), f32)
        c2 = jnp.zeros((8, E), f32)
        for r0 in range(lo, hi, CH):
            rows = pl.ds(r0, CH)
            e = jnp.exp2(e_ref[sl, rows, :] * mul - SHIFT * LOG2E)
            e_ref[sl, rows, :] = e
            q1 = e * e
            u = e * UP
            q2 = u * u
            c1 = c1 + jnp.sum(q1.reshape(CH // 8, 8, E), axis=0)
            c2 = c2 + jnp.sum(q2.reshape(CH // 8, 8, E), axis=0)
            r1 = (q1[:, 0:128] + q1[:, 128:256]) + (q1[:, 256:384] + q1[:, 384:512])
            r2 = (q2[:, 0:128] + q2[:, 128:256]) + (q2[:, 256:384] + q2[:, 384:512])
            if not first:
                r1 = r1 + racc_ref[0, rows, :]
                r2 = r2 + racc_ref[1, rows, :]
            racc_ref[0, rows, :] = r1
            racc_ref[1, rows, :] = r2
        if lo > 0:
            c1 = c1 + cacc_ref[0, :, pl.ds(sl * E, E)]
            c2 = c2 + cacc_ref[1, :, pl.ds(sl * E, E)]
        cacc_ref[0, :, pl.ds(sl * E, E)] = c1
        cacc_ref[1, :, pl.ds(sl * E, E)] = c2

    for k in (2, -2):
        sis[k % NZ].wait_recv()
        transpose_a(arow(k, 1))
    logits(0, 0, NEAR)
    ring_step(3)
    for k in (3, -3):
        transpose_a(arow(k, 0))
    pcopy.wait_recv()
    for q in range(NZ * 2):
        prow_ref[pl.ds(q * R, R), :] = jnp.broadcast_to(
            part_ref[q % 2, ORDER[q // 2]][0:1, :], (R, R)).T

    order = (0, 1, 3, 2)
    for n, sl in enumerate(order):
        if n + 1 < NX:
            logits(order[n + 1], 0, NEAR)
        exponentials(sl, 0, NEAR, n == 0)
    for k in (3, -3):
        sis[k % NZ].wait_recv()
        transpose_a(arow(k, 1))
    up[0].wait_recv()
    down[1].wait_recv()
    to_sister(4)
    transpose_a(arow(4, 0))
    sis[4].wait_recv()
    transpose_a(arow(4, 1))
    logits(order[0], NEAR, TR)
    for n, sl in enumerate(order):
        if n + 1 < NX:
            logits(order[n + 1], NEAR, TR)
        exponentials(sl, NEAR, TR, n == 0)

    def local_lse(s1, s2):
        return jnp.where(
            s1 > DOWN, jnp.log(s1) + 2.0 * SHIFT, jnp.log(s2) - 2.0 * SHIFT)

    def combine(parts):
        top = parts[0]
        for p in parts[1:]:
            top = jnp.maximum(top, p)
        total = jnp.exp(parts[0] - top)
        for p in parts[1:]:
            total = total + jnp.exp(p - top)
        return top + jnp.log(total)

    def abs_row(q):
        return lax.rem(z + ORDER[q // 2], NZ) * 2 + lax.rem(c + q % 2, 2)

    def abs_col(p):
        return lax.rem(x + p // NY, NX) * NY + lax.rem(y + p % NY, NY)

    col = local_lse(
        jnp.sum(cacc_ref[0], axis=0, keepdims=True), jnp.sum(cacc_ref[1], axis=0, keepdims=True))
    for p in range(16):
        csnd_ref[pl.ds(abs_col(p), 1), :] = col[:, p * R : (p + 1) * R]
    cmsg = [
        send(csnd_ref, crcv_ref.at[n], dev(dx=i, dy=j)) for n, (i, j) in enumerate(plane)
    ]
    ones = jnp.ones((8, R), bf16)

    def row_sum(k):
        v = racc_ref[k]
        hi = v.astype(bf16)
        lo = (v - hi.astype(f32)).astype(bf16)
        return dot_nt(ones, hi) + dot_nt(ones, lo)

    row = local_lse(row_sum(0), row_sum(1))
    for q in range(16):
        rsnd_ref[pl.ds(abs_row(q), 1), :] = row[0:1, q * R : (q + 1) * R]
    rmsg = [send(rsnd_ref, rrcv_ref.at[d - 1], dev(dz=d)) for d in range(1, NZ)]
    for copy in cmsg:
        copy.wait_recv()
    lse_col = combine([csnd_ref[...]] + [crcv_ref[n] for n in range(len(plane))])
    root = jnp.sqrt(jnp.full((16, R), scale * 0.5, f32))
    lses_ref[0] = lse_col
    cfac_ref[...] = jnp.exp(SHIFT - 0.5 * lse_col) * root
    for p in range(16):
        cst_ref[:, pl.ds(p * R, R)] = jnp.broadcast_to(
            cfac_ref[pl.ds(abs_col(p), 1), :], (8, R))
    for copy in rmsg:
        copy.wait_recv()
    lse_row = combine([rsnd_ref[...]] + [rrcv_ref[d] for d in range(NZ - 1)])
    rhalf_ref[0] = lse_row
    rcopy = send(rhalf_ref.at[0], rhalf_ref.at[1], dev(dc=1))
    rcopy.wait_recv()
    lse_row = combine([lse_row, rhalf_ref[1]])
    lses_ref[1] = lse_row
    rfac_ref[...] = jnp.exp(SHIFT - 0.5 * lse_row) * root
    for q in range(16):
        rrow_ref[pl.ds(q * R, R), :] = jnp.broadcast_to(
            rfac_ref[pl.ds(abs_row(q), 1), :], (R, R)).T
    own_lse = lses_ref[0, pl.ds(abs_col(0), 1), :] + lses_ref[1, pl.ds(abs_row(0), 1), :]

    h0, h1, qmsg, zmsg, done = {}, {}, {}, {}, set()
    zin = {1: zp_ref, -1: zm_ref}

    def gradient(sl, d):
        d = d % NZ
        if (sl, d) in done:
            return
        done.add((sl, d))
        for r0 in range(arow(d, 0), arow(d, 0) + HALF, CH):
            rows = pl.ds(r0, CH)
            rr = rrow_ref[rows, :].reshape(CH // 8, 8, R)
            pr = prow_ref[rows, :].reshape(CH // 8, 8, R)
            pos = None
            for lg in range(NY):
                cols = pl.ds(sl * E + lg * R, R)
                e = e_ref[sl, rows, pl.ds(lg * R, R)].reshape(CH // 8, 8, R)
                u = e * rr
                v = e * cst_ref[:, cols][None]
                hit = pr == cid_ref[:, cols][None]
                g = u * u + v * v - jnp.where(hit, scale, 0.0)
                pe = jnp.where(hit, e, 0.0)
                pos = pe if pos is None else pos + pe
                g_ref[sl, rows, pl.ds(lg * R, R)] = g.reshape(CH, R).astype(bf16)
            pos = pos.reshape(CH, R)
            if sl != 2:
                pos = pos + pacc_ref[rows, :]
            pacc_ref[rows, :] = pos

    def slab(sl):
        gbt_ref[sl] = dot_nn(at_ref[...], g_ref[sl]).astype(bf16)

    def slab_send(sl):
        if sl:
            h0[sl] = send(gbt_ref.at[sl, pl.ds(0, HALF)], rh0_ref.at[sl - 1], dev(dx=sl))
        for dy in (2, 1, 3):
            h1[sl, dy] = send(
                gbt_ref.at[sl, pl.ds(HALF, HALF), pl.ds(dy * R, R)],
                rh1_ref.at[dy - 1, sl], dev(dy=dy))

    def radar(d):
        total = None
        for sl in range(NX):
            t = dot_nn(g_ref[sl, pl.ds(arow(d, 0), HALF), :], b_ref[pl.ds(sl * E, E), :])
            total = t if total is None else total + t
        qown_ref[d % NZ] = total[0:R]
        qsis_ref[d % NZ] = total[R:].astype(bf16)

    def radar_send(d):
        qmsg[d % NZ] = send(qsis_ref.at[d % NZ], qrcv_ref.at[d % NZ], dev(dc=1))

    def chip_sum(d):
        qmsg[d % NZ].wait_recv()
        return qown_ref[d % NZ] + qrcv_ref[d % NZ].astype(f32)

    def ring(k):
        q = {1: chip_sum(k), -1: chip_sum(-k)}
        for h in range(2):
            for sign in (1, -1):
                d = (sign * k) % NZ
                v = q[sign][:, h * HALF : (h + 1) * HALF]
                if k < 3 or h == (0 if sign > 0 else 1):
                    zmsg[sign, h].wait_recv()
                    v = v + zin[sign][3 - k, h].astype(f32)
                qsnd_ref[d, h] = v.astype(bf16)
                zmsg[sign, h] = send(
                    qsnd_ref.at[d, h], zin[sign].at[4 - k, h], dev(dz=sign))

    def rows_of(*ds):
        for d in ds:
            for sl in (1, 3, 0):
                gradient(sl, d)

    def col_of(sl):
        for d in range(NZ):
            gradient(sl, d)

    col_of(2)
    slab(2)
    rows_of(4)
    slab_send(2)
    radar(4)
    rows_of(3)
    radar_send(4)
    radar(3)
    rows_of(-3)
    radar_send(3)
    radar(-3)
    col_of(1)
    radar_send(-3)
    q4 = chip_sum(4).astype(bf16)
    for h, sign in ((0, 1), (1, -1)):
        qsnd_ref[4, h] = q4[:, h * HALF : (h + 1) * HALF]
        zmsg[sign, h] = send(qsnd_ref.at[4, h], zin[sign].at[0, h], dev(dz=sign))
    slab(1)
    rows_of(2, -2)
    slab_send(1)
    radar(2)
    radar(-2)
    col_of(3)
    radar_send(2)
    radar_send(-2)
    ring(3)
    slab(3)
    col_of(0)
    slab_send(3)
    slab(0)
    slab_send(0)
    radar(1)
    radar(-1)
    radar_send(1)
    radar_send(-1)
    radar(0)
    radar_send(0)
    ring(2)

    pos = pacc_ref[...]
    pos = jnp.where(pos > 0.0, 2.0 * (jnp.log(jnp.where(pos > 0.0, pos, 1.0)) + SHIFT), 0.0)
    pos = jnp.sum(pos.reshape(TR // 8, 8, R), axis=0)
    row0 = lax.broadcasted_iota(jnp.int32, (8, R), 0) == 0
    both = jnp.broadcast_to(own_lse, (8, R))
    lr_ref[0] = jnp.where(row0, both, 0.0) - 2.0 * pos
    lmsg = [send(lr_ref.at[0], lr_ref.at[NX - d], dev(dx=d)) for d in range(1, NX)]

    def gather_loss(first, n, me, msgs):
        for copy in msgs:
            copy.wait_recv()
        t = jnp.zeros((8, R), f32)
        for i in range(n):
            t = t + lr_ref[first + lax.rem(i - me + n, n)]
        return t

    ring(1)

    t0 = gbt_ref[0, pl.ds(0, HALF), :].astype(f32)
    for d in (2, 1, 3):
        h0[d].wait_recv()
        t0 = t0 + rh0_ref[d - 1].astype(f32)
    th0_ref[...] = t0.astype(bf16)
    p2a = [
        send(th0_ref.at[:, pl.ds(d * R, R)], p2h0_ref.at[d - 1], dev(dy=d)) for d in range(1, NY)
    ]
    gh0 = t0[:, :R]
    p2b = []
    for sl in (2, 1, 3, 0):
        t1 = gbt_ref[sl, pl.ds(HALF, HALF), pl.ds(0, R)].astype(f32)
        for d in (2, 1, 3):
            h1[sl, d].wait_recv()
            t1 = t1 + rh1_ref[d - 1, sl].astype(f32)
        if sl:
            th1_ref[sl] = t1.astype(bf16)
            p2b.append(send(th1_ref.at[sl], p2h1_ref.at[sl - 1], dev(dx=sl)))
        else:
            gh1 = t1

    def unproject(grad_unit, raw_ref, inv):
        raw = raw_ref[...]
        inner = jnp.sum(raw * grad_unit, axis=1, keepdims=True)
        return (inv * grad_unit - raw * (inv * inv * inv * inner)).astype(bf16)

    def head_exchange(t, grad):
        gsnd_ref[t] = jnp.where(core0, grad[:, HALF:], grad[:, :HALF])
        gmine_ref[t] = jnp.where(core0, grad[:, :HALF], grad[:, HALF:])
        return send(gsnd_ref.at[t], grcv_ref.at[t], dev(dc=1))

    def head_first(t, copy):
        copy.wait_recv()
        w = dot_nn(ft_ref[t, :, pl.ds(0, R)], gmine_ref[t]) + dot_nn(
            ft_ref[t, :, pl.ds(R, R)], grcv_ref[t])
        w = w.reshape(NZ, NX, NY, 8, HALF)
        for ix in range(NX):
            for iy in range(NY):
                v = w[:, ix, iy].reshape(NZ * 8, HALF).astype(bf16)
                sx_ref[t, ix, pl.ds(iy * 64, 64), :] = v[:, :R]
                sy_ref[t, iy, pl.ds(ix * 64, 64), :] = v[:, R:]
        out = []
        for d in (2, 1, 3):
            out.append(send(sx_ref.at[t, lax.rem(x + d, NX)], rx_ref.at[t, d - 1], dev(dx=d)))
            out.append(send(sy_ref.at[t, lax.rem(y + d, NY)], ry_ref.at[t, d - 1], dev(dy=d)))
        return out

    def head_second(t, msgs):
        tx = sx_ref[t, x].astype(f32)
        ty = sy_ref[t, y].astype(f32)
        for copy in msgs:
            copy.wait_recv()
        for d in range(3):
            tx = tx + rx_ref[t, d].astype(f32)
            ty = ty + ry_ref[t, d].astype(f32)
        sx2_ref[t] = tx.astype(bf16).reshape(NY, 64, R)
        sy2_ref[t] = ty.astype(bf16).reshape(NX, 64, R)
        out = []
        for d in (2, 1, 3):
            out.append(send(sx2_ref.at[t, lax.rem(y + d, NY)], rx2_ref.at[t, d - 1], dev(dy=d)))
            out.append(send(sy2_ref.at[t, lax.rem(x + d, NX)], ry2_ref.at[t, d - 1], dev(dx=d)))
        return out

    def head_third(t, msgs):
        tx = sx2_ref[t, y].astype(f32)
        ty = sy2_ref[t, x].astype(f32)
        for copy in msgs:
            copy.wait_recv()
        for d in range(3):
            tx = tx + rx2_ref[t, d].astype(f32)
            ty = ty + ry2_ref[t, d].astype(f32)
        u_ref[t, :, :, pl.ds(0, R)] = tx.reshape(NZ, 8, R)
        u_ref[t, :, :, pl.ds(R, R)] = ty.reshape(NZ, 8, R)
        return [
            send(u_ref.at[t, lax.rem(z + d, NZ)], rz_ref.at[t, d - 1], dev(dz=d))
            for d in (4, 3, 5, 2, 6, 1, 7)
        ]

    def head_fourth(t, msgs):
        total = u_ref[t, z]
        for copy in msgs:
            copy.wait_recv()
        for d in range(NZ - 1):
            total = total + rz_ref[t, d]
        fin_ref[t] = total
        return send(fin_ref.at[t], sis_ref.at[t], dev(dc=1))

    def head_out(t, copy, out_ref):
        copy.wait_recv()
        own = fin_ref[t]
        other = sis_ref[t]
        out_ref[:, pl.ds(0, HALF)] = jnp.where(core0, own[0:4], other[4:8])
        out_ref[:, pl.ds(HALF, HALF)] = jnp.where(core0, other[0:4], own[4:8])

    q0 = chip_sum(0)
    halves = []
    for h in range(2):
        zmsg[1, h].wait_recv()
        zmsg[-1, h].wait_recv()
        halves.append(
            q0[:, h * HALF : (h + 1) * HALF]
            + (zp_ref[3, h].astype(f32) + zm_ref[3, h].astype(f32)))
    grs = unproject(jnp.concatenate(halves, axis=1), raws_ref, inv_s)
    smsg = head_exchange(0, grs)
    lr_ref[4] = gather_loss(0, NX, x, lmsg)
    lmsg = [send(lr_ref.at[4], lr_ref.at[4 + NY - d], dev(dy=d)) for d in range(1, NY)]
    smsg = head_first(0, smsg)

    for copy in p2a + p2b:
        copy.wait_recv()
    for d in range(NX - 1):
        gh0 = gh0 + p2h0_ref[d].astype(f32)
        gh1 = gh1 + p2h1_ref[d].astype(f32)
    gro = unproject(jnp.concatenate([gh0.T, gh1.T], axis=1), rawo_ref, inv_o)
    omsg = head_exchange(1, gro)
    gsar_ref[...] = dot_nt(grs, ws_ref[...]).astype(bf16)
    omsg = head_first(1, omsg)
    gopt_ref[...] = dot_nt(gro, wo_ref[...]).astype(bf16)
    lr_ref[8] = gather_loss(4, NY, y, lmsg)
    lmsg = [send(lr_ref.at[8], lr_ref.at[8 + NZ - d], dev(dz=d)) for d in range(1, NZ)]
    smsg = head_second(0, smsg)
    omsg = head_second(1, omsg)
    lr_ref[16] = gather_loss(8, NZ, z, lmsg)
    lmsg = [send(lr_ref.at[16], lr_ref.at[17], dev(dc=1))]
    smsg = head_third(0, smsg)
    omsg = head_third(1, omsg)
    loss_ref[0] = jnp.sum(gather_loss(16, 2, c, lmsg)) * (1.0 / (2.0 * NX * NY * NZ * 2 * R))
    smsg = head_fourth(0, smsg)
    omsg = head_fourth(1, omsg)
    head_out(0, smsg, gws_ref)
    head_out(1, omsg, gwo_ref)

    for copy in sent:
        copy.wait_send()


def local(sar_feats, opt_feats, w_sar, w_opt, logit_scale, partner):
    V = pltpu.VMEM
    scratch = [
        V((TR, E), bf16), V((E, TR), bf16), V((TC, E), bf16),
        V((NX, TR, E), f32), V((NX, TR, E), bf16), V((R, E), f32), V((R, E), f32),
        V((2, NZ, 8, R), f32), V((TR, R), f32), V((8, TC), f32),
        V((2, TR, R), f32), V((2, 8, TC), f32), V((TR, R), f32),
        V((16, R), f32), V((16, R), f32), V((NZ - 1, 16, R), f32), V((15, 16, R), f32),
        V((2, 16, R), f32), V((16, R), f32), V((16, R), f32), V((2, 16, R), f32),
        V((8, TC), f32), V((TR, R), f32), V((NX, E, E), bf16), V((3, HALF, E), bf16), V((3, NX, HALF, R), bf16),
        V((HALF, E), bf16), V((NX, HALF, R), bf16), V((3, HALF, R), bf16), V((3, HALF, R), bf16),
        V((NZ, R, E), f32), V((NZ, R, E), bf16), V((NZ, R, E), bf16), V((NZ, 2, R, HALF), bf16),
        V((4, 2, R, HALF), bf16), V((4, 2, R, HALF), bf16),
        V((2, R, F), bf16), V((2, F, 2 * R), bf16),
        V((2, R, HALF), bf16), V((2, R, HALF), bf16), V((2, R, HALF), bf16),
        V((2, NX, HALF, R), bf16), V((2, NY, HALF, R), bf16),
        V((2, 3, HALF, R), bf16), V((2, 3, HALF, R), bf16),
        V((2, NY, 64, R), bf16), V((2, NX, 64, R), bf16),
        V((2, 3, 64, R), bf16), V((2, 3, 64, R), bf16),
        V((2, NZ, 8, HALF), f32), V((2, NZ - 1, 8, HALF), f32),
        V((2, 8, HALF), f32), V((2, 8, HALF), f32),
        V((18, 8, R), f32),
        pltpu.SemaphoreType.DMA((MSGS,)), pltpu.SemaphoreType.DMA((MSGS,)),
    ]
    vm = pl.BlockSpec(memory_space=pltpu.VMEM)
    sm = pl.BlockSpec(memory_space=pltpu.SMEM)
    shapes = (
        jax.ShapeDtypeStruct((1,), f32),
        jax.ShapeDtypeStruct((R, F), bf16),
        jax.ShapeDtypeStruct((R, F), bf16),
        jax.ShapeDtypeStruct((4, E), f32),
        jax.ShapeDtypeStruct((4, E), f32),
    )
    outs = pl.pallas_call(
        kernel,
        out_shape=shapes,
        in_specs=[vm, vm, vm, vm, sm, vm],
        out_specs=(sm, vm, vm, vm, vm),
        scratch_shapes=scratch,
        compiler_params=pltpu.CompilerParams(
            collective_id=0, has_side_effects=True, vmem_limit_bytes=62 * 1024 * 1024),
        name="contrastive",
    )(sar_feats, opt_feats, w_sar, w_opt, logit_scale, partner.reshape(NY * 2, R))
    return pl.pallas_call(
        hand_over,
        out_shape=shapes,
        in_specs=[sm, vm, vm, vm, vm],
        out_specs=(sm, vm, vm, vm, vm),
        name="hand_over",
    )(*outs)


def hand_over(l_in, a_in, b_in, c_in, d_in, l_out, a_out, b_out, c_out, d_out):
    l_out[0] = l_in[0]
    for i, o in ((a_in, a_out), (b_in, b_out), (c_in, c_out), (d_in, d_out)):
        o[...] = i[...]


def solution(mesh):
    return jax.shard_map(
        local,
        mesh=mesh,
        in_specs=(
            P(("wide", "narrow"), None),
            P(("wide", "narrow"), None),
            P(),
            P(),
            P(),
            P("wide"),
        ),
        out_specs=(
            P(),
            P(("wide", "narrow"), None),
            P(("wide", "narrow"), None),
            P(("wide", "narrow"), None),
            P(("wide", "narrow"), None),
        ),
        check_vma=False,
    )
```

```python
import jax
import jax.numpy as jnp
from jax import lax
from jax.experimental import pallas as pl
from jax.experimental.pallas import tpu as pltpu
from jax.sharding import PartitionSpec as P

NX, NY, NZ = 4, 4, 8
R = 128
E = 512
F = 1024
HALF = 256
TR = NZ * 2 * R
TC = NX * NY * R
LOG2E = 1.4426950408889634
SHIFT = 25.0
UP = 5.184705528587072e21
DOWN = 1.9287498e-22
MSGS = 256
ORDER = (0, 1, 7, 2, 6, 3, 5, 4)
NEAR = 5 * 2 * R
f32 = jnp.float32
bf16 = jnp.bfloat16
MESH = pl.DeviceIdType.MESH


def dot_nt(a, b):
    return lax.dot_general(a, b, (((1,), (1,)), ((), ())), preferred_element_type=f32)


def dot_nn(a, b):
    return jnp.dot(a, b, preferred_element_type=f32)


def kernel(
    sar_in, opt_in, ws_in, wo_in, scale_ref, partner_ref,
    loss_ref, gsar_ref, gopt_ref, gws_ref, gwo_ref,
    a_ref, at_ref, b_ref, e_ref, g_ref, raws_ref, rawo_ref,
    part_ref, prow_ref, cid_ref, racc_ref, cacc_ref, pacc_ref,
    rsnd_ref, csnd_ref, rrcv_ref, crcv_ref, lses_ref, cfac_ref, rfac_ref, rhalf_ref,
    cst_ref, rrow_ref, gbt_ref, rh0_ref, rh1_ref, th0_ref, th1_ref, p2h0_ref, p2h1_ref,
    qown_ref, qsis_ref, qrcv_ref, qsnd_ref, zp_ref, zm_ref,
    frcv_ref, ft_ref, gmine_ref, gsnd_ref, grcv_ref,
    sx_ref, sy_ref, rx_ref, ry_ref, sx2_ref, sy2_ref, rx2_ref, ry2_ref,
    u_ref, rz_ref, fin_ref, sis_ref, lr_ref,
    sar_ref, opt_ref, ws_ref, wo_ref, ssem, rsem, lsem,
):
    wide = lax.axis_index("wide")
    narrow = lax.axis_index("narrow")
    x, y, z, c = lax.rem(wide, NX), narrow // 2, wide // NX, lax.rem(narrow, 2)

    def dev(dx=0, dy=0, dz=0, dc=0):
        px = lax.rem(x + (dx % NX), NX)
        py = lax.rem(y + (dy % NY), NY)
        pz = lax.rem(z + (dz % NZ), NZ)
        pc = lax.rem(c + (dc % 2), 2)
        return (pz * NX + px, py * 2 + pc)

    plane = [(i, j) for i in range(NX) for j in range(NY) if (i, j) != (0, 0)]

    barrier = pltpu.get_barrier_semaphore()
    for i, j in plane:
        pl.semaphore_signal(barrier, inc=1, device_id=dev(dx=i, dy=j), device_id_type=MESH)
    for i in range(1, NZ):
        pl.semaphore_signal(barrier, inc=1, device_id=dev(dz=i), device_id_type=MESH)
    pl.semaphore_signal(barrier, inc=1, device_id=dev(dc=1), device_id_type=MESH)

    loads = []
    for n, (src, dst) in enumerate(
        ((opt_in, opt_ref), (wo_in, wo_ref), (sar_in, sar_ref), (ws_in, ws_ref))
    ):
        copy = pltpu.make_async_copy(src, dst, lsem.at[n])
        copy.start()
        loads.append(copy)

    sent = []
    settled = []
    early = []

    def sent_off(copy):
        copy.wait_send()
        early.append(copy)

    def settle(upto):
        while len(settled) < upto:
            copy = sent[len(settled)]
            if not any(copy is e for e in early):
                copy.wait_send()
            settled.append(True)

    def send(src, dst, device):
        m = len(sent)
        copy = pltpu.make_async_remote_copy(
            src_ref=src, dst_ref=dst, send_sem=ssem.at[m], recv_sem=rsem.at[m],
            device_id=device, device_id_type=MESH,
        )
        copy.start()
        sent.append(copy)
        return copy

    def brow(dx, dy):
        return ((dx % NX) * NY + (dy % NY)) * R

    def arow(dz, dc):
        return (ORDER.index(dz % NZ) * 2 + dc % 2) * R

    scale = scale_ref[0]

    def project(feat_ref, w_ref, raw_ref, dst_ref):
        raw = dot_nn(feat_ref[...], w_ref[...])
        inv = lax.rsqrt(jnp.sum(raw * raw, axis=1, keepdims=True) + 1e-06)
        raw_ref[...] = raw
        dst_ref[pl.ds(0, R), :] = (raw * inv).astype(bf16)
        return inv

    loads[0].wait()
    loads[1].wait()
    inv_o = project(opt_ref, wo_ref, rawo_ref, b_ref)
    loads[2].wait()
    loads[3].wait()
    inv_s = project(sar_ref, ws_ref, raws_ref, a_ref)
    own_partner = partner_ref[pl.ds(narrow, 1), :].astype(f32)
    part_ref[0, 0] = jnp.broadcast_to(own_partner, (8, R))
    core0 = c == 0

    pl.semaphore_wait(barrier, len(plane) + NZ)

    bx, by, late, sis = {}, {}, {}, {}
    own_b = b_ref.at[pl.ds(0, R)]
    lanes = [pl.ds(0, HALF), pl.ds(HALF, HALF)]

    def zsend(h, src, dst, sign):
        return send(
            a_ref.at[pl.ds(arow(src, 0), R), lanes[h]],
            a_ref.at[pl.ds(arow(dst, 0), R), lanes[h]], dev(dz=sign))

    up = [zsend(h, 0, -1, 1) for h in range(2)]
    down = [zsend(h, 0, 1, -1) for h in range(2)]
    for d in (1, 3, 2):
        bx[d] = send(own_b, b_ref.at[pl.ds(brow(-d, 0), R)], dev(dx=d))
        by[d] = send(own_b, b_ref.at[pl.ds(brow(0, -d), R)], dev(dy=d))

    def to_sister(d):
        sis[d % NZ] = send(
            a_ref.at[pl.ds(arow(d, 0), R)], a_ref.at[pl.ds(arow(d, 1), R)], dev(dc=1))

    to_sister(0)
    parts = [
        send(part_ref.at[0, 0], part_ref.at[0, (-i) % NZ], dev(dz=i)) for i in range(1, NZ)
    ]
    sar = sar_ref[...]
    opt = opt_ref[...]
    fcopy = [
        send(sar_ref, frcv_ref.at[0], dev(dc=1)), send(opt_ref, frcv_ref.at[1], dev(dc=1))
    ]
    lane = lax.broadcasted_iota(jnp.int32, (8, R), 1)
    for i in range(NX):
        for j in range(NY):
            wx = z * NX + lax.rem(x + i, NX)
            ny = lax.rem(y + j, NY) * 2 + c
            base = (wx * (NY * 2) + ny) * R
            cid_ref[:, pl.ds(brow(i, j), R)] = (lane + base).astype(f32)

    def transpose_a(row):
        at_ref[:, pl.ds(row, R)] = a_ref[pl.ds(row, R), :].T

    def ring_step(k):
        for h in range(2):
            up[h].wait_recv()
            if k < 3 or h == 0:
                up[h] = zsend(h, -k, -k - 1, 1)
            down[h].wait_recv()
            if k < 3 or h == 1:
                down[h] = zsend(h, k, k + 1, -1)
        to_sister(-k)
        to_sister(k)

    def plane_step(d):
        bx[d].wait_recv()
        for dy in (1, 3, 2):
            late[(-d) % NX, (-dy) % NY, 0] = send(
                b_ref.at[pl.ds(brow(-d, 0), R), lanes[0]],
                b_ref.at[pl.ds(brow(-d, -dy), R), lanes[0]], dev(dy=dy))
        by[d].wait_recv()
        for dx in (1, 3, 2):
            late[(-dx) % NX, (-d) % NY, 1] = send(
                b_ref.at[pl.ds(brow(0, -d), R), lanes[1]],
                b_ref.at[pl.ds(brow(-dx, -d), R), lanes[1]], dev(dx=dx))

    ring_step(1)
    plane_step(1)
    plane_step(3)
    for k in (0, 1, -1):
        transpose_a(arow(k, 0))
    ft_ref[0, :, pl.ds(0, R)] = sar.T
    ft_ref[1, :, pl.ds(0, R)] = opt.T
    plane_step(2)
    ring_step(2)
    for k in (2, -2):
        transpose_a(arow(k, 0))
    for t in range(2):
        fcopy[t].wait_recv()
        ft_ref[t, :, pl.ds(R, R)] = frcv_ref[t].T
    for copy in parts:
        copy.wait_recv()
    pcopy = send(part_ref.at[0], part_ref.at[1], dev(dc=1))
    for k in (0, 1, -1):
        sis[k % NZ].wait_recv()
        transpose_a(arow(k, 1))
    mul = scale * (0.5 * LOG2E)
    CH = 64

    def logits(sl, lo):
        for i, j, h in sorted(late):
            if i == sl and lo == 0:
                late[i, j, h].wait_recv()
        return dot_nt(a_ref[pl.ds(lo, HALF), :], b_ref[pl.ds(sl * E, E), :])

    def exponentials(sl, lo, value):
        c1 = jnp.zeros((8, E), f32)
        c2 = jnp.zeros((8, E), f32)
        for r0 in range(0, HALF, CH):
            rows = pl.ds(lo + r0, CH)
            e = jnp.exp2(value[r0 : r0 + CH] * mul - SHIFT * LOG2E)
            e_ref[sl, rows, :] = e
            q1 = e * e
            u = e * UP
            q2 = u * u
            c1 = c1 + jnp.sum(q1.reshape(CH // 8, 8, E), axis=0)
            c2 = c2 + jnp.sum(q2.reshape(CH // 8, 8, E), axis=0)
            r1 = (q1[:, 0:128] + q1[:, 128:256]) + (q1[:, 256:384] + q1[:, 384:512])
            r2 = (q2[:, 0:128] + q2[:, 128:256]) + (q2[:, 256:384] + q2[:, 384:512])
            if sl > 0:
                r1 = r1 + racc_ref[0, rows, :]
                r2 = r2 + racc_ref[1, rows, :]
            racc_ref[0, rows, :] = r1
            racc_ref[1, rows, :] = r2
        if lo > 0:
            c1 = c1 + cacc_ref[0, :, pl.ds(sl * E, E)]
            c2 = c2 + cacc_ref[1, :, pl.ds(sl * E, E)]
        cacc_ref[0, :, pl.ds(sl * E, E)] = c1
        cacc_ref[1, :, pl.ds(sl * E, E)] = c2

    def tiles(lo, hi, *slabs):
        todo = [(sl, r0) for sl in slabs for r0 in range(lo, hi, HALF)]
        value = logits(*todo[0])
        for n, tile in enumerate(todo):
            ahead = logits(*todo[n + 1]) if n + 1 < len(todo) else None
            exponentials(*tile, value)
            value = ahead

    for k in (2, -2):
        sis[k % NZ].wait_recv()
        transpose_a(arow(k, 1))
    tiles(0, 3 * HALF, 0)
    ring_step(3)
    for k in (3, -3):
        transpose_a(arow(k, 0))
    pcopy.wait_recv()
    for q in range(NZ * 2):
        prow_ref[pl.ds(q * R, R), :] = jnp.broadcast_to(
            part_ref[q % 2, ORDER[q // 2]][0:1, :], (R, R)).T

    def local_lse(s1, s2):
        return jnp.where(
            s1 > DOWN, jnp.log(s1) + 2.0 * SHIFT, jnp.log(s2) - 2.0 * SHIFT)

    ones = jnp.ones((8, R), bf16)

    def row_sum(k, lo, hi):
        v = racc_ref[k, pl.ds(lo, hi - lo), :]
        top = v.astype(bf16)
        rest = (v - top.astype(f32)).astype(bf16)
        return dot_nt(ones, top) + dot_nt(ones, rest)

    tiles(3 * HALF, NEAR, 0)
    tiles(0, NEAR, 1)
    up[0].wait_recv()
    down[1].wait_recv()
    to_sister(4)
    transpose_a(arow(4, 0))
    for k in (3, -3):
        sis[k % NZ].wait_recv()
        transpose_a(arow(k, 1))
    tiles(0, NEAR, 3, 2)
    near_row = local_lse(row_sum(0, 0, NEAR), row_sum(1, 0, NEAR))
    sis[4].wait_recv()
    transpose_a(arow(4, 1))
    gathered = len(sent)
    tiles(NEAR, TR, 0, 1, 3, 2)

    def combine(parts):
        top = parts[0]
        for p in parts[1:]:
            top = jnp.maximum(top, p)
        total = jnp.exp(parts[0] - top)
        for p in parts[1:]:
            total = total + jnp.exp(p - top)
        return top + jnp.log(total)

    def abs_row(q):
        return lax.rem(z + ORDER[q // 2], NZ) * 2 + lax.rem(c + q % 2, 2)

    def abs_col(p):
        return lax.rem(x + p // NY, NX) * NY + lax.rem(y + p % NY, NY)

    far_row = local_lse(row_sum(0, NEAR, TR), row_sum(1, NEAR, TR))
    for q in range(16):
        v = near_row[0:1, q * R : (q + 1) * R] if q < 10 else far_row[
            0:1, (q - 10) * R : (q - 9) * R]
        rsnd_ref[pl.ds(abs_row(q), 1), :] = v
    rmsg = [send(rsnd_ref, rrcv_ref.at[d - 1], dev(dz=d)) for d in range(1, NZ)]
    col = local_lse(
        jnp.sum(cacc_ref[0], axis=0, keepdims=True), jnp.sum(cacc_ref[1], axis=0, keepdims=True))
    for p in range(16):
        csnd_ref[pl.ds(abs_col(p), 1), :] = col[:, p * R : (p + 1) * R]
    cmsg = [
        send(csnd_ref, crcv_ref.at[n], dev(dx=i, dy=j)) for n, (i, j) in enumerate(plane)
    ]
    settle(gathered)
    for copy in cmsg:
        copy.wait_recv()
    lse_col = combine([csnd_ref[...]] + [crcv_ref[n] for n in range(len(plane))])
    root = jnp.sqrt(jnp.full((16, R), scale * 0.5, f32))
    lses_ref[0] = lse_col
    cfac_ref[...] = jnp.exp(SHIFT - 0.5 * lse_col) * root
    for p in range(16):
        cst_ref[:, pl.ds(p * R, R)] = jnp.broadcast_to(
            cfac_ref[pl.ds(abs_col(p), 1), :], (8, R))
    for copy in rmsg:
        copy.wait_recv()
    lse_row = combine([rsnd_ref[...]] + [rrcv_ref[d] for d in range(NZ - 1)])
    rhalf_ref[0] = lse_row
    rcopy = send(rhalf_ref.at[0], rhalf_ref.at[1], dev(dc=1))
    rcopy.wait_recv()
    lse_row = combine([lse_row, rhalf_ref[1]])
    lses_ref[1] = lse_row
    rfac_ref[...] = jnp.exp(SHIFT - 0.5 * lse_row) * root
    for q in range(16):
        rrow_ref[pl.ds(q * R, R), :] = jnp.broadcast_to(
            rfac_ref[pl.ds(abs_row(q), 1), :], (R, R)).T
    own_lse = lses_ref[0, pl.ds(abs_col(0), 1), :] + lses_ref[1, pl.ds(abs_row(0), 1), :]

    h0, h1, qmsg, zmsg, done = {}, {}, {}, {}, set()
    zin = {1: zp_ref, -1: zm_ref}

    def gradient(sl, d):
        d = d % NZ
        if (sl, d) in done:
            return
        done.add((sl, d))
        for r0 in range(arow(d, 0), arow(d, 0) + HALF, CH):
            rows = pl.ds(r0, CH)
            rr = rrow_ref[rows, :].reshape(CH // 8, 8, R)
            pr = prow_ref[rows, :].reshape(CH // 8, 8, R)
            pos = None
            for lg in range(NY):
                cols = pl.ds(sl * E + lg * R, R)
                e = e_ref[sl, rows, pl.ds(lg * R, R)].reshape(CH // 8, 8, R)
                u = e * rr
                v = e * cst_ref[:, cols][None]
                hit = pr == cid_ref[:, cols][None]
                g = u * u + v * v - jnp.where(hit, scale, 0.0)
                pe = jnp.where(hit, e, 0.0)
                pos = pe if pos is None else pos + pe
                g_ref[rows, cols] = g.reshape(CH, R).astype(bf16)
            pos = pos.reshape(CH, R)
            if sl != 2:
                pos = pos + pacc_ref[rows, :]
            pacc_ref[rows, :] = pos

    def slab(sl):
        gbt_ref[sl] = dot_nn(at_ref[...], g_ref[:, pl.ds(sl * E, E)]).astype(bf16)

    def slab_send(sl):
        if sl:
            h0[sl] = send(gbt_ref.at[sl, pl.ds(0, HALF)], rh0_ref.at[sl - 1], dev(dx=sl))
        for dy in (2, 1, 3):
            h1[sl, dy] = send(
                gbt_ref.at[sl, pl.ds(HALF, HALF), pl.ds(dy * R, R)],
                rh1_ref.at[dy - 1, sl], dev(dy=dy))

    def radar(*ds):
        rows = pl.ds(arow(ds[0], 0), len(ds) * HALF)
        total = dot_nn(g_ref[rows, :], b_ref[...])
        for n, d in enumerate(ds):
            qown_ref[d % NZ] = total[n * HALF : n * HALF + R]
            qsis_ref[d % NZ] = total[n * HALF + R : (n + 1) * HALF].astype(bf16)

    def radar_send(d):
        qmsg[d % NZ] = send(qsis_ref.at[d % NZ], qrcv_ref.at[d % NZ], dev(dc=1))

    def chip_sum(d):
        qmsg[d % NZ].wait_recv()
        return qown_ref[d % NZ] + qrcv_ref[d % NZ].astype(f32)

    def ring(k, chain):
        for sign in (1, -1):
            h = chain if sign > 0 else 1 - chain
            d = (sign * k) % NZ
            v = qown_ref[d, :, lanes[h]] + qrcv_ref[d, :, lanes[h]].astype(f32)
            if k < 3 or (k == 3 and chain == 0):
                zmsg[sign, h].wait_recv()
                v = v + zin[sign][3 - k, h].astype(f32)
            qsnd_ref[d, h] = v.astype(bf16)
            zmsg[sign, h] = send(qsnd_ref.at[d, h], zin[sign].at[4 - k, h], dev(dz=sign))

    def arrived(*ds):
        for d in ds:
            qmsg[d % NZ].wait_recv()

    def rows_of(*ds):
        for d in ds:
            for sl in (1, 3, 0):
                gradient(sl, d)

    def col_of(sl):
        for d in range(NZ):
            gradient(sl, d)

    stats = len(sent)
    col_of(2)
    slab(2)
    rows_of(4)
    slab_send(2)
    radar(4)
    rows_of(3, -3)
    radar_send(4)
    radar(3, -3)
    col_of(1)
    radar_send(3)
    radar_send(-3)
    arrived(4)
    ring(4, 0)
    slab(1)
    rows_of(2, -2)
    arrived(3, -3)
    ring(3, 1)
    slab_send(1)
    radar(2, -2)
    col_of(3)
    radar_send(2)
    radar_send(-2)
    ring(3, 0)
    slab(3)
    col_of(0)
    slab_send(3)
    arrived(2, -2)
    ring(2, 1)
    slab(0)
    slab_send(0)
    ring(2, 0)
    radar(1, -1)
    radar_send(1)
    radar_send(-1)
    radar(0)
    radar_send(0)
    arrived(1, -1)
    ring(1, 1)
    ring(1, 0)
    reduced = len(sent)
    settle(stats)

    pos = pacc_ref[...]
    pos = jnp.where(pos > 0.0, 2.0 * (jnp.log(jnp.where(pos > 0.0, pos, 1.0)) + SHIFT), 0.0)
    pos = jnp.sum(pos.reshape(TR // 8, 8, R), axis=0)
    row0 = lax.broadcasted_iota(jnp.int32, (8, R), 0) == 0
    both = jnp.broadcast_to(own_lse, (8, R))
    lr_ref[0] = jnp.where(row0, both, 0.0) - 2.0 * pos
    lmsg = [send(lr_ref.at[0], lr_ref.at[NX - d], dev(dx=d)) for d in range(1, NX)]

    def gather_loss(first, n, me, msgs):
        for copy in msgs:
            copy.wait_recv()
        t = jnp.zeros((8, R), f32)
        for i in range(n):
            t = t + lr_ref[first + lax.rem(i - me + n, n)]
        return t


    t0 = gbt_ref[0, pl.ds(0, HALF), :].astype(f32)
    for d in (2, 1, 3):
        h0[d].wait_recv()
        t0 = t0 + rh0_ref[d - 1].astype(f32)
    th0_ref[...] = t0.astype(bf16)
    p2a = [
        send(th0_ref.at[:, pl.ds(d * R, R)], p2h0_ref.at[d - 1], dev(dy=d)) for d in range(1, NY)
    ]
    gh0 = t0[:, :R]
    p2b = []
    for sl in (2, 1, 3, 0):
        t1 = gbt_ref[sl, pl.ds(HALF, HALF), pl.ds(0, R)].astype(f32)
        for d in (2, 1, 3):
            h1[sl, d].wait_recv()
            t1 = t1 + rh1_ref[d - 1, sl].astype(f32)
        if sl:
            th1_ref[sl] = t1.astype(bf16)
            p2b.append(send(th1_ref.at[sl], p2h1_ref.at[sl - 1], dev(dx=sl)))
        else:
            gh1 = t1

    def unproject(grad_unit, raw_ref, inv):
        raw = raw_ref[...]
        inner = jnp.sum(raw * grad_unit, axis=1, keepdims=True)
        return (inv * grad_unit - raw * (inv * inv * inv * inner)).astype(bf16)

    def head_exchange(t, grad):
        gsnd_ref[t] = jnp.where(core0, grad[:, HALF:], grad[:, :HALF])
        gmine_ref[t] = jnp.where(core0, grad[:, :HALF], grad[:, HALF:])
        return send(gsnd_ref.at[t], grcv_ref.at[t], dev(dc=1))

    def head_first(t, copy):
        copy.wait_recv()
        w = dot_nn(ft_ref[t, :, pl.ds(0, R)], gmine_ref[t]) + dot_nn(
            ft_ref[t, :, pl.ds(R, R)], grcv_ref[t])
        w = w.reshape(NZ, NX, NY, 8, HALF)
        for ix in range(NX):
            for iy in range(NY):
                v = w[:, ix, iy].reshape(NZ * 8, HALF).astype(bf16)
                sx_ref[t, ix, pl.ds(iy * 64, 64), :] = v[:, :R]
                sy_ref[t, iy, pl.ds(ix * 64, 64), :] = v[:, R:]
        out = []
        for d in (2, 1, 3):
            out.append(send(sx_ref.at[t, lax.rem(x + d, NX)], rx_ref.at[t, d - 1], dev(dx=d)))
            out.append(send(sy_ref.at[t, lax.rem(y + d, NY)], ry_ref.at[t, d - 1], dev(dy=d)))
        return out

    def head_second(t, msgs):
        tx = sx_ref[t, x].astype(f32)
        ty = sy_ref[t, y].astype(f32)
        for copy in msgs:
            copy.wait_recv()
        for d in range(3):
            tx = tx + rx_ref[t, d].astype(f32)
            ty = ty + ry_ref[t, d].astype(f32)
        sx2_ref[t] = tx.astype(bf16).reshape(NY, 64, R)
        sy2_ref[t] = ty.astype(bf16).reshape(NX, 64, R)
        out = []
        for d in (2, 1, 3):
            out.append(send(sx2_ref.at[t, lax.rem(y + d, NY)], rx2_ref.at[t, d - 1], dev(dy=d)))
            out.append(send(sy2_ref.at[t, lax.rem(x + d, NX)], ry2_ref.at[t, d - 1], dev(dx=d)))
        return out

    def head_third(t, msgs):
        tx = sx2_ref[t, y].astype(f32)
        ty = sy2_ref[t, x].astype(f32)
        for copy in msgs:
            copy.wait_recv()
        for d in range(3):
            tx = tx + rx2_ref[t, d].astype(f32)
            ty = ty + ry2_ref[t, d].astype(f32)
        u_ref[t, :, :, pl.ds(0, R)] = tx.reshape(NZ, 8, R)
        u_ref[t, :, :, pl.ds(R, R)] = ty.reshape(NZ, 8, R)
        return [
            send(u_ref.at[t, lax.rem(z + d, NZ)], rz_ref.at[t, d - 1], dev(dz=d))
            for d in (4, 3, 5, 2, 6, 1, 7)
        ]

    def head_fourth(t, msgs):
        total = u_ref[t, z]
        for copy in msgs:
            copy.wait_recv()
        for d in range(NZ - 1):
            total = total + rz_ref[t, d]
        fin_ref[t] = total
        return send(fin_ref.at[t], sis_ref.at[t], dev(dc=1))

    def head_out(t, copy, out_ref):
        copy.wait_recv()
        own = fin_ref[t]
        other = sis_ref[t]
        out_ref[:, pl.ds(0, HALF)] = jnp.where(core0, own[0:4], other[4:8])
        out_ref[:, pl.ds(HALF, HALF)] = jnp.where(core0, other[0:4], own[4:8])

    settle(reduced)
    q0 = chip_sum(0)
    halves = []
    for h in range(2):
        zmsg[1, h].wait_recv()
        zmsg[-1, h].wait_recv()
        halves.append(
            q0[:, h * HALF : (h + 1) * HALF]
            + (zp_ref[3, h].astype(f32) + zm_ref[3, h].astype(f32)))
    grs = unproject(jnp.concatenate(halves, axis=1), raws_ref, inv_s)
    smsg = head_exchange(0, grs)
    lr_ref[4] = gather_loss(0, NX, x, lmsg)
    lmsg = [send(lr_ref.at[4], lr_ref.at[4 + NY - d], dev(dy=d)) for d in range(1, NY)]
    smsg = head_first(0, smsg)

    for copy in p2a + p2b:
        copy.wait_recv()
    for d in range(NX - 1):
        gh0 = gh0 + p2h0_ref[d].astype(f32)
        gh1 = gh1 + p2h1_ref[d].astype(f32)
    gro = unproject(jnp.concatenate([gh0.T, gh1.T], axis=1), rawo_ref, inv_o)
    omsg = head_exchange(1, gro)
    omsg = head_first(1, omsg)
    gsar_ref[...] = dot_nt(grs, ws_ref[...]).astype(bf16)
    gopt_ref[...] = dot_nt(gro, wo_ref[...]).astype(bf16)
    lr_ref[8] = gather_loss(4, NY, y, lmsg)
    lmsg = [send(lr_ref.at[8], lr_ref.at[8 + NZ - d], dev(dz=d)) for d in range(1, NZ)]
    heads = len(sent)
    smsg = head_second(0, smsg)
    omsg = head_second(1, omsg)
    lr_ref[16] = gather_loss(8, NZ, z, lmsg)
    lmsg = [send(lr_ref.at[16], lr_ref.at[17], dev(dc=1))]
    smsg = head_third(0, smsg)
    omsg = head_third(1, omsg)
    loss_ref[0] = jnp.sum(gather_loss(16, 2, c, lmsg)) * (1.0 / (2.0 * NX * NY * NZ * 2 * R))
    settle(heads)
    smsg = head_fourth(0, smsg)
    omsg = head_fourth(1, omsg)
    head_out(0, smsg, gws_ref)
    head_out(1, omsg, gwo_ref)

    settle(len(sent))


def local(sar_feats, opt_feats, w_sar, w_opt, logit_scale, partner):
    V = pltpu.VMEM
    scratch = [
        V((TR, E), bf16), V((E, TR), bf16), V((TC, E), bf16),
        V((NX, TR, E), f32), V((TR, TC), bf16), V((R, E), f32), V((R, E), f32),
        V((2, NZ, 8, R), f32), V((TR, R), f32), V((8, TC), f32),
        V((2, TR, R), f32), V((2, 8, TC), f32), V((TR, R), f32),
        V((16, R), f32), V((16, R), f32), V((NZ - 1, 16, R), f32), V((15, 16, R), f32),
        V((2, 16, R), f32), V((16, R), f32), V((16, R), f32), V((2, 16, R), f32),
        V((8, TC), f32), V((TR, R), f32), V((NX, E, E), bf16), V((3, HALF, E), bf16), V((3, NX, HALF, R), bf16),
        V((HALF, E), bf16), V((NX, HALF, R), bf16), V((3, HALF, R), bf16), V((3, HALF, R), bf16),
        V((NZ, R, E), f32), V((NZ, R, E), bf16), V((NZ, R, E), bf16), V((NZ, 2, R, HALF), bf16),
        V((4, 2, R, HALF), bf16), V((4, 2, R, HALF), bf16),
        V((2, R, F), bf16), V((2, F, 2 * R), bf16),
        V((2, R, HALF), bf16), V((2, R, HALF), bf16), V((2, R, HALF), bf16),
        V((2, NX, HALF, R), bf16), V((2, NY, HALF, R), bf16),
        V((2, 3, HALF, R), bf16), V((2, 3, HALF, R), bf16),
        V((2, NY, 64, R), bf16), V((2, NX, 64, R), bf16),
        V((2, 3, 64, R), bf16), V((2, 3, 64, R), bf16),
        V((2, NZ, 8, HALF), f32), V((2, NZ - 1, 8, HALF), f32),
        V((2, 8, HALF), f32), V((2, 8, HALF), f32),
        V((18, 8, R), f32),
        V((R, F), bf16), V((R, F), bf16), V((F, E), bf16), V((F, E), bf16),
        pltpu.SemaphoreType.DMA((MSGS,)), pltpu.SemaphoreType.DMA((MSGS,)),
        pltpu.SemaphoreType.DMA((4,)),
    ]
    vm = pl.BlockSpec(memory_space=pltpu.VMEM)
    hb = pl.BlockSpec(memory_space=pl.ANY)
    sm = pl.BlockSpec(memory_space=pltpu.SMEM)
    shapes = (
        jax.ShapeDtypeStruct((1,), f32),
        jax.ShapeDtypeStruct((R, F), bf16),
        jax.ShapeDtypeStruct((R, F), bf16),
        jax.ShapeDtypeStruct((4, E), f32),
        jax.ShapeDtypeStruct((4, E), f32),
    )
    outs = pl.pallas_call(
        kernel,
        out_shape=shapes,
        in_specs=[hb, hb, hb, hb, sm, vm],
        out_specs=(sm, vm, vm, vm, vm),
        scratch_shapes=scratch,
        compiler_params=pltpu.CompilerParams(
            collective_id=0, has_side_effects=True, vmem_limit_bytes=62 * 1024 * 1024),
        name="contrastive",
    )(sar_feats, opt_feats, w_sar, w_opt, logit_scale, partner.reshape(NY * 2, R))
    return pl.pallas_call(
        hand_over,
        out_shape=shapes,
        in_specs=[sm, vm, vm, vm, vm],
        out_specs=(sm, vm, vm, vm, vm),
        name="hand_over",
    )(*outs)


def hand_over(l_in, a_in, b_in, c_in, d_in, l_out, a_out, b_out, c_out, d_out):
    l_out[0] = l_in[0]
    for i, o in ((a_in, a_out), (b_in, b_out), (c_in, c_out), (d_in, d_out)):
        o[...] = i[...]


def solution(mesh):
    return jax.shard_map(
        local,
        mesh=mesh,
        in_specs=(
            P(("wide", "narrow"), None),
            P(("wide", "narrow"), None),
            P(),
            P(),
            P(),
            P("wide"),
        ),
        out_specs=(
            P(),
            P(("wide", "narrow"), None),
            P(("wide", "narrow"), None),
            P(("wide", "narrow"), None),
            P(("wide", "narrow"), None),
        ),
        check_vma=False,
    )
```

```python
import jax
import jax.numpy as jnp
from jax import lax
from jax.experimental import pallas as pl
from jax.experimental.pallas import tpu as pltpu
from jax.sharding import PartitionSpec as P

NX, NY, NZ = 4, 4, 8
R = 128
E = 512
F = 1024
HALF = 256
TR = NZ * 2 * R
TC = NX * NY * R
LOG2E = 1.4426950408889634
SHIFT = 25.0
UP = 5.184705528587072e21
DOWN = 1.9287498e-22
MSGS = 256
ORDER = (0, 1, 7, 2, 6, 3, 5, 4)
NEAR = 5 * 2 * R
f32 = jnp.float32
bf16 = jnp.bfloat16
MESH = pl.DeviceIdType.MESH


def dot_nt(a, b):
    return lax.dot_general(a, b, (((1,), (1,)), ((), ())), preferred_element_type=f32)


def dot_nn(a, b):
    return jnp.dot(a, b, preferred_element_type=f32)


def kernel(
    sar_in, opt_in, ws_in, wo_in, scale_ref, partner_ref,
    loss_ref, gsar_ref, gopt_ref, gws_ref, gwo_ref,
    a_ref, at_ref, b_ref, e_ref, g_ref, raws_ref, rawo_ref,
    part_ref, prow_ref, cid_ref, racc_ref, cacc_ref, pacc_ref,
    rsnd_ref, csnd_ref, rrcv_ref, crcv_ref, lses_ref, cfac_ref, rfac_ref, rhalf_ref,
    cst_ref, rrow_ref, gbt_ref, rh0_ref, rh1_ref, th0_ref, th1_ref, p2h0_ref, p2h1_ref,
    qown_ref, qsis_ref, qrcv_ref, qsnd_ref, zp_ref, zm_ref,
    frcv_ref, ft_ref, gmine_ref, gsnd_ref, grcv_ref,
    sx_ref, sy_ref, rx_ref, ry_ref, sx2_ref, sy2_ref, rx2_ref, ry2_ref,
    u_ref, rz_ref, fin_ref, sis_ref, lr_ref,
    sar_ref, opt_ref, ws_ref, wo_ref, ssem, rsem, lsem,
):
    wide = lax.axis_index("wide")
    narrow = lax.axis_index("narrow")
    x, y, z, c = lax.rem(wide, NX), narrow // 2, wide // NX, lax.rem(narrow, 2)

    def dev(dx=0, dy=0, dz=0, dc=0):
        px = lax.rem(x + (dx % NX), NX)
        py = lax.rem(y + (dy % NY), NY)
        pz = lax.rem(z + (dz % NZ), NZ)
        pc = lax.rem(c + (dc % 2), 2)
        return (pz * NX + px, py * 2 + pc)

    plane = [(i, j) for i in range(NX) for j in range(NY) if (i, j) != (0, 0)]

    barrier = pltpu.get_barrier_semaphore()
    for i, j in plane:
        pl.semaphore_signal(barrier, inc=1, device_id=dev(dx=i, dy=j), device_id_type=MESH)
    for i in range(1, NZ):
        pl.semaphore_signal(barrier, inc=1, device_id=dev(dz=i), device_id_type=MESH)
    pl.semaphore_signal(barrier, inc=1, device_id=dev(dc=1), device_id_type=MESH)

    loads = []
    for n, (src, dst) in enumerate(
        ((opt_in, opt_ref), (wo_in, wo_ref), (sar_in, sar_ref), (ws_in, ws_ref))
    ):
        copy = pltpu.make_async_copy(src, dst, lsem.at[n])
        copy.start()
        loads.append(copy)

    sent = []
    settled = []
    early = []

    def sent_off(copy):
        copy.wait_send()
        early.append(copy)

    def settle(upto):
        while len(settled) < upto:
            copy = sent[len(settled)]
            if not any(copy is e for e in early):
                copy.wait_send()
            settled.append(True)

    def send(src, dst, device):
        m = len(sent)
        copy = pltpu.make_async_remote_copy(
            src_ref=src, dst_ref=dst, send_sem=ssem.at[m], recv_sem=rsem.at[m],
            device_id=device, device_id_type=MESH,
        )
        copy.start()
        sent.append(copy)
        return copy

    def brow(dx, dy):
        return ((dx % NX) * NY + (dy % NY)) * R

    def arow(dz, dc):
        return (ORDER.index(dz % NZ) * 2 + dc % 2) * R

    scale = scale_ref[0]

    def project(feat_ref, w_ref, raw_ref, dst_ref):
        raw = dot_nn(feat_ref[...], w_ref[...])
        inv = lax.rsqrt(jnp.sum(raw * raw, axis=1, keepdims=True) + 1e-06)
        raw_ref[...] = raw
        dst_ref[pl.ds(0, R), :] = (raw * inv).astype(bf16)
        return inv

    loads[0].wait()
    loads[1].wait()
    inv_o = project(opt_ref, wo_ref, rawo_ref, b_ref)
    loads[2].wait()
    loads[3].wait()
    inv_s = project(sar_ref, ws_ref, raws_ref, a_ref)
    own_partner = partner_ref[pl.ds(narrow, 1), :].astype(f32)
    part_ref[0, 0] = jnp.broadcast_to(own_partner, (8, R))
    core0 = c == 0

    pl.semaphore_wait(barrier, len(plane) + NZ)

    bx, by, late, sis = {}, {}, {}, {}
    own_b = b_ref.at[pl.ds(0, R)]
    lanes = [pl.ds(0, HALF), pl.ds(HALF, HALF)]

    def zsend(h, src, dst, sign):
        return send(
            a_ref.at[pl.ds(arow(src, 0), R), lanes[h]],
            a_ref.at[pl.ds(arow(dst, 0), R), lanes[h]], dev(dz=sign))

    up = [zsend(h, 0, -1, 1) for h in range(2)]
    down = [zsend(h, 0, 1, -1) for h in range(2)]
    for d in (1, 3, 2):
        bx[d] = send(own_b, b_ref.at[pl.ds(brow(-d, 0), R)], dev(dx=d))
        by[d] = send(own_b, b_ref.at[pl.ds(brow(0, -d), R)], dev(dy=d))

    def to_sister(d):
        sis[d % NZ] = send(
            a_ref.at[pl.ds(arow(d, 0), R)], a_ref.at[pl.ds(arow(d, 1), R)], dev(dc=1))

    to_sister(0)
    parts = [
        send(part_ref.at[0, 0], part_ref.at[0, (-i) % NZ], dev(dz=i)) for i in range(1, NZ)
    ]
    sar = sar_ref[...]
    opt = opt_ref[...]
    fcopy = [
        send(sar_ref, frcv_ref.at[0], dev(dc=1)), send(opt_ref, frcv_ref.at[1], dev(dc=1))
    ]
    lane = lax.broadcasted_iota(jnp.int32, (8, R), 1)
    for i in range(NX):
        for j in range(NY):
            wx = z * NX + lax.rem(x + i, NX)
            ny = lax.rem(y + j, NY) * 2 + c
            base = (wx * (NY * 2) + ny) * R
            cid_ref[:, pl.ds(brow(i, j), R)] = (lane + base).astype(f32)

    def transpose_a(row):
        at_ref[:, pl.ds(row, R)] = a_ref[pl.ds(row, R), :].T

    def ring_step(k):
        for h in range(2):
            up[h].wait_recv()
            if k < 3 or h == 0:
                up[h] = zsend(h, -k, -k - 1, 1)
            down[h].wait_recv()
            if k < 3 or h == 1:
                down[h] = zsend(h, k, k + 1, -1)
        to_sister(-k)
        to_sister(k)

    def plane_step(d):
        bx[d].wait_recv()
        for dy in (1, 3, 2):
            late[(-d) % NX, (-dy) % NY, 0] = send(
                b_ref.at[pl.ds(brow(-d, 0), R), lanes[0]],
                b_ref.at[pl.ds(brow(-d, -dy), R), lanes[0]], dev(dy=dy))
        by[d].wait_recv()
        for dx in (1, 3, 2):
            late[(-dx) % NX, (-d) % NY, 1] = send(
                b_ref.at[pl.ds(brow(0, -d), R), lanes[1]],
                b_ref.at[pl.ds(brow(-dx, -d), R), lanes[1]], dev(dx=dx))

    ring_step(1)
    plane_step(1)
    plane_step(3)
    for k in (0, 1, -1):
        transpose_a(arow(k, 0))
    ft_ref[0, :, pl.ds(0, R)] = sar.T
    ft_ref[1, :, pl.ds(0, R)] = opt.T
    plane_step(2)
    ring_step(2)
    for k in (2, -2):
        transpose_a(arow(k, 0))
    for t in range(2):
        fcopy[t].wait_recv()
        ft_ref[t, :, pl.ds(R, R)] = frcv_ref[t].T
    for copy in parts:
        copy.wait_recv()
    pcopy = send(part_ref.at[0], part_ref.at[1], dev(dc=1))
    for k in (0, 1, -1):
        sis[k % NZ].wait_recv()
        transpose_a(arow(k, 1))
    mul = scale * (0.5 * LOG2E)
    CH = 64

    def logits(sl, lo):
        for i, j, h in sorted(late):
            if i == sl and lo == 0:
                late[i, j, h].wait_recv()
        return dot_nt(a_ref[pl.ds(lo, HALF), :], b_ref[pl.ds(sl * E, E), :])

    def exponentials(sl, lo, value):
        c1 = jnp.zeros((8, E), f32)
        c2 = jnp.zeros((8, E), f32)
        for r0 in range(0, HALF, CH):
            rows = pl.ds(lo + r0, CH)
            e = jnp.exp2(value[r0 : r0 + CH] * mul - SHIFT * LOG2E)
            e_ref[sl, rows, :] = e
            q1 = e * e
            u = e * UP
            q2 = u * u
            c1 = c1 + jnp.sum(q1.reshape(CH // 8, 8, E), axis=0)
            c2 = c2 + jnp.sum(q2.reshape(CH // 8, 8, E), axis=0)
            r1 = (q1[:, 0:128] + q1[:, 128:256]) + (q1[:, 256:384] + q1[:, 384:512])
            r2 = (q2[:, 0:128] + q2[:, 128:256]) + (q2[:, 256:384] + q2[:, 384:512])
            if sl > 0:
                r1 = r1 + racc_ref[0, rows, :]
                r2 = r2 + racc_ref[1, rows, :]
            racc_ref[0, rows, :] = r1
            racc_ref[1, rows, :] = r2
        if lo > 0:
            c1 = c1 + cacc_ref[0, :, pl.ds(sl * E, E)]
            c2 = c2 + cacc_ref[1, :, pl.ds(sl * E, E)]
        cacc_ref[0, :, pl.ds(sl * E, E)] = c1
        cacc_ref[1, :, pl.ds(sl * E, E)] = c2

    def tiles(lo, hi, *slabs):
        todo = [(sl, r0) for sl in slabs for r0 in range(lo, hi, HALF)]
        value = logits(*todo[0])
        for n, tile in enumerate(todo):
            ahead = logits(*todo[n + 1]) if n + 1 < len(todo) else None
            exponentials(*tile, value)
            value = ahead

    for k in (2, -2):
        sis[k % NZ].wait_recv()
        transpose_a(arow(k, 1))
    tiles(0, 3 * HALF, 0)
    ring_step(3)
    for k in (3, -3):
        transpose_a(arow(k, 0))
    pcopy.wait_recv()
    for q in range(NZ * 2):
        prow_ref[pl.ds(q * R, R), :] = jnp.broadcast_to(
            part_ref[q % 2, ORDER[q // 2]][0:1, :], (R, R)).T

    def local_lse(s1, s2):
        return jnp.where(
            s1 > DOWN, jnp.log(s1) + 2.0 * SHIFT, jnp.log(s2) - 2.0 * SHIFT)

    ones = jnp.ones((8, R), bf16)

    def row_sum(k, lo, hi):
        v = racc_ref[k, pl.ds(lo, hi - lo), :]
        top = v.astype(bf16)
        rest = (v - top.astype(f32)).astype(bf16)
        return dot_nt(ones, top) + dot_nt(ones, rest)

    tiles(3 * HALF, NEAR, 0)
    tiles(0, NEAR, 1)
    up[0].wait_recv()
    down[1].wait_recv()
    to_sister(4)
    transpose_a(arow(4, 0))
    for k in (3, -3):
        sis[k % NZ].wait_recv()
        transpose_a(arow(k, 1))
    tiles(0, NEAR, 3, 2)
    near_row = local_lse(row_sum(0, 0, NEAR), row_sum(1, 0, NEAR))
    sis[4].wait_recv()
    transpose_a(arow(4, 1))
    gathered = len(sent)
    tiles(NEAR, TR, 0, 1, 3, 2)

    def combine(parts):
        top = parts[0]
        for p in parts[1:]:
            top = jnp.maximum(top, p)
        total = jnp.exp(parts[0] - top)
        for p in parts[1:]:
            total = total + jnp.exp(p - top)
        return top + jnp.log(total)

    def abs_row(q):
        return lax.rem(z + ORDER[q // 2], NZ) * 2 + lax.rem(c + q % 2, 2)

    def abs_col(p):
        return lax.rem(x + p // NY, NX) * NY + lax.rem(y + p % NY, NY)

    far_row = local_lse(row_sum(0, NEAR, TR), row_sum(1, NEAR, TR))
    for q in range(16):
        v = near_row[0:1, q * R : (q + 1) * R] if q < 10 else far_row[
            0:1, (q - 10) * R : (q - 9) * R]
        rsnd_ref[pl.ds(abs_row(q), 1), :] = v
    rmsg = [send(rsnd_ref, rrcv_ref.at[d - 1], dev(dz=d)) for d in range(1, NZ)]
    col = local_lse(
        jnp.sum(cacc_ref[0], axis=0, keepdims=True), jnp.sum(cacc_ref[1], axis=0, keepdims=True))
    for p in range(16):
        csnd_ref[pl.ds(abs_col(p), 1), :] = col[:, p * R : (p + 1) * R]
    cmsg = [
        send(csnd_ref, crcv_ref.at[n], dev(dx=i, dy=j)) for n, (i, j) in enumerate(plane)
    ]
    settle(gathered)
    for copy in cmsg:
        copy.wait_recv()
    lse_col = combine([csnd_ref[...]] + [crcv_ref[n] for n in range(len(plane))])
    root = jnp.sqrt(jnp.full((16, R), scale * 0.5, f32))
    lses_ref[0] = lse_col
    cfac_ref[...] = jnp.exp(SHIFT - 0.5 * lse_col) * root
    for p in range(16):
        cst_ref[:, pl.ds(p * R, R)] = jnp.broadcast_to(
            cfac_ref[pl.ds(abs_col(p), 1), :], (8, R))
    for copy in rmsg:
        copy.wait_recv()
    lse_row = combine([rsnd_ref[...]] + [rrcv_ref[d] for d in range(NZ - 1)])
    rhalf_ref[0] = lse_row
    rcopy = send(rhalf_ref.at[0], rhalf_ref.at[1], dev(dc=1))
    rcopy.wait_recv()
    lse_row = combine([lse_row, rhalf_ref[1]])
    lses_ref[1] = lse_row
    rfac_ref[...] = jnp.exp(SHIFT - 0.5 * lse_row) * root
    for q in range(16):
        rrow_ref[pl.ds(q * R, R), :] = jnp.broadcast_to(
            rfac_ref[pl.ds(abs_row(q), 1), :], (R, R)).T
    own_lse = lses_ref[0, pl.ds(abs_col(0), 1), :] + lses_ref[1, pl.ds(abs_row(0), 1), :]

    h0, h1, qmsg, zmsg, done = {}, {}, {}, {}, set()
    zin = {1: zp_ref, -1: zm_ref}

    def gradient(sl, d):
        d = d % NZ
        if (sl, d) in done:
            return
        done.add((sl, d))
        for r0 in range(arow(d, 0), arow(d, 0) + HALF, CH):
            rows = pl.ds(r0, CH)
            rr = rrow_ref[rows, :].reshape(CH // 8, 8, R)
            pr = prow_ref[rows, :].reshape(CH // 8, 8, R)
            pos = None
            for lg in range(NY):
                cols = pl.ds(sl * E + lg * R, R)
                e = e_ref[sl, rows, pl.ds(lg * R, R)].reshape(CH // 8, 8, R)
                u = e * rr
                v = e * cst_ref[:, cols][None]
                hit = pr == cid_ref[:, cols][None]
                g = u * u + v * v - jnp.where(hit, scale, 0.0)
                pe = jnp.where(hit, e, 0.0)
                pos = pe if pos is None else pos + pe
                g_ref[rows, cols] = g.reshape(CH, R).astype(bf16)
            pos = pos.reshape(CH, R)
            if sl != 2:
                pos = pos + pacc_ref[rows, :]
            pacc_ref[rows, :] = pos

    def slab(sl):
        gbt_ref[sl] = dot_nn(at_ref[...], g_ref[:, pl.ds(sl * E, E)]).astype(bf16)

    def slab_send(sl):
        if sl:
            h0[sl] = send(gbt_ref.at[sl, pl.ds(0, HALF)], rh0_ref.at[sl - 1], dev(dx=sl))
        for dy in (2, 1, 3):
            h1[sl, dy] = send(
                gbt_ref.at[sl, pl.ds(HALF, HALF), pl.ds(dy * R, R)],
                rh1_ref.at[dy - 1, sl], dev(dy=dy))

    def radar(*ds):
        rows = pl.ds(arow(ds[0], 0), len(ds) * HALF)
        total = dot_nn(g_ref[rows, :], b_ref[...])
        for n, d in enumerate(ds):
            qown_ref[d % NZ] = total[n * HALF : n * HALF + R]
            qsis_ref[d % NZ] = total[n * HALF + R : (n + 1) * HALF].astype(bf16)

    def radar_send(d):
        qmsg[d % NZ] = send(qsis_ref.at[d % NZ], qrcv_ref.at[d % NZ], dev(dc=1))

    def chip_sum(d):
        qmsg[d % NZ].wait_recv()
        return qown_ref[d % NZ] + qrcv_ref[d % NZ].astype(f32)

    def ring(k, chain):
        for sign in (1, -1):
            h = chain if sign > 0 else 1 - chain
            d = (sign * k) % NZ
            v = qown_ref[d, :, lanes[h]] + qrcv_ref[d, :, lanes[h]].astype(f32)
            if k < 3 or (k == 3 and chain == 0):
                zmsg[sign, h].wait_recv()
                v = v + zin[sign][3 - k, h].astype(f32)
            qsnd_ref[d, h] = v.astype(bf16)
            zmsg[sign, h] = send(qsnd_ref.at[d, h], zin[sign].at[4 - k, h], dev(dz=sign))

    def arrived(*ds):
        for d in ds:
            qmsg[d % NZ].wait_recv()

    def rows_of(*ds):
        for d in ds:
            for sl in (1, 3, 0):
                gradient(sl, d)

    def col_of(sl):
        for d in range(NZ):
            gradient(sl, d)

    stats = len(sent)
    col_of(2)
    slab(2)
    rows_of(4)
    slab_send(2)
    radar(4)
    rows_of(3, -3)
    radar_send(4)
    radar(3, -3)
    col_of(1)
    radar_send(3)
    radar_send(-3)
    arrived(4)
    ring(4, 0)
    slab(1)
    rows_of(2, -2)
    arrived(3, -3)
    ring(3, 1)
    slab_send(1)
    radar(2, -2)
    col_of(3)
    radar_send(2)
    radar_send(-2)
    ring(3, 0)
    slab(3)
    col_of(0)
    slab_send(3)
    arrived(2, -2)
    ring(2, 1)
    slab(0)
    slab_send(0)
    ring(2, 0)
    radar(1, -1)
    radar_send(1)
    radar_send(-1)
    radar(0)
    radar_send(0)
    arrived(1, -1)
    ring(1, 1)
    ring(1, 0)
    reduced = len(sent)
    settle(stats)

    pos = pacc_ref[...]
    pos = jnp.where(pos > 0.0, 2.0 * (jnp.log(jnp.where(pos > 0.0, pos, 1.0)) + SHIFT), 0.0)
    pos = jnp.sum(pos.reshape(TR // 8, 8, R), axis=0)
    row0 = lax.broadcasted_iota(jnp.int32, (8, R), 0) == 0
    both = jnp.broadcast_to(own_lse, (8, R))
    lr_ref[0] = jnp.where(row0, both, 0.0) - 2.0 * pos
    lmsg = [send(lr_ref.at[0], lr_ref.at[NX - d], dev(dx=d)) for d in range(1, NX)]

    def gather_loss(first, n, me, msgs):
        for copy in msgs:
            copy.wait_recv()
        t = jnp.zeros((8, R), f32)
        for i in range(n):
            t = t + lr_ref[first + lax.rem(i - me + n, n)]
        return t


    t0 = gbt_ref[0, pl.ds(0, HALF), :].astype(f32)
    for d in (2, 1, 3):
        h0[d].wait_recv()
        t0 = t0 + rh0_ref[d - 1].astype(f32)
    th0_ref[...] = t0.astype(bf16)
    p2a = [
        send(th0_ref.at[:, pl.ds(d * R, R)], p2h0_ref.at[d - 1], dev(dy=d)) for d in range(1, NY)
    ]
    gh0 = t0[:, :R]
    p2b = []
    for sl in (2, 1, 3, 0):
        t1 = gbt_ref[sl, pl.ds(HALF, HALF), pl.ds(0, R)].astype(f32)
        for d in (2, 1, 3):
            h1[sl, d].wait_recv()
            t1 = t1 + rh1_ref[d - 1, sl].astype(f32)
        if sl:
            th1_ref[sl] = t1.astype(bf16)
            p2b.append(send(th1_ref.at[sl], p2h1_ref.at[sl - 1], dev(dx=sl)))
        else:
            gh1 = t1

    def unproject(grad_unit, raw_ref, inv):
        raw = raw_ref[...]
        inner = jnp.sum(raw * grad_unit, axis=1, keepdims=True)
        return (inv * grad_unit - raw * (inv * inv * inv * inner)).astype(bf16)

    def head_exchange(t, grad):
        gsnd_ref[t] = jnp.where(core0, grad[:, HALF:], grad[:, :HALF])
        gmine_ref[t] = jnp.where(core0, grad[:, :HALF], grad[:, HALF:])
        return send(gsnd_ref.at[t], grcv_ref.at[t], dev(dc=1))

    def head_first(t, copy):
        copy.wait_recv()
        w = dot_nn(ft_ref[t, :, pl.ds(0, R)], gmine_ref[t]) + dot_nn(
            ft_ref[t, :, pl.ds(R, R)], grcv_ref[t])
        w = w.reshape(NZ, NX, NY, 8, HALF)
        for ix in range(NX):
            for iy in range(NY):
                v = w[:, ix, iy].reshape(NZ * 8, HALF).astype(bf16)
                sx_ref[t, ix, pl.ds(iy * 64, 64), :] = v[:, :R]
                sy_ref[t, iy, pl.ds(ix * 64, 64), :] = v[:, R:]
        out = []
        for d in (2, 1, 3):
            out.append(send(sx_ref.at[t, lax.rem(x + d, NX)], rx_ref.at[t, d - 1], dev(dx=d)))
            out.append(send(sy_ref.at[t, lax.rem(y + d, NY)], ry_ref.at[t, d - 1], dev(dy=d)))
        return out

    def head_second(t, msgs):
        tx = sx_ref[t, x].astype(f32)
        ty = sy_ref[t, y].astype(f32)
        for copy in msgs:
            copy.wait_recv()
        for d in range(3):
            tx = tx + rx_ref[t, d].astype(f32)
            ty = ty + ry_ref[t, d].astype(f32)
        sx2_ref[t] = tx.astype(bf16).reshape(NY, 64, R)
        sy2_ref[t] = ty.astype(bf16).reshape(NX, 64, R)
        out = []
        for d in (2, 1, 3):
            out.append(send(sx2_ref.at[t, lax.rem(y + d, NY)], rx2_ref.at[t, d - 1], dev(dy=d)))
            out.append(send(sy2_ref.at[t, lax.rem(x + d, NX)], ry2_ref.at[t, d - 1], dev(dx=d)))
        return out

    def head_third(t, msgs):
        tx = sx2_ref[t, y].astype(f32)
        ty = sy2_ref[t, x].astype(f32)
        for copy in msgs:
            copy.wait_recv()
        for d in range(3):
            tx = tx + rx2_ref[t, d].astype(f32)
            ty = ty + ry2_ref[t, d].astype(f32)
        u_ref[t, :, :, pl.ds(0, R)] = tx.reshape(NZ, 8, R)
        u_ref[t, :, :, pl.ds(R, R)] = ty.reshape(NZ, 8, R)
        return [
            send(u_ref.at[t, lax.rem(z + d, NZ)], rz_ref.at[t, d - 1], dev(dz=d))
            for d in (4, 3, 5, 2, 6, 1, 7)
        ]

    def head_fourth(t, msgs):
        total = u_ref[t, z]
        for copy in msgs:
            copy.wait_recv()
        for d in range(NZ - 1):
            total = total + rz_ref[t, d]
        fin_ref[t] = total
        return send(fin_ref.at[t], sis_ref.at[t], dev(dc=1))

    def head_out(t, copy, out_ref):
        copy.wait_recv()
        own = fin_ref[t]
        other = sis_ref[t]
        out_ref[:, pl.ds(0, HALF)] = jnp.where(core0, own[0:4], other[4:8])
        out_ref[:, pl.ds(HALF, HALF)] = jnp.where(core0, other[0:4], own[4:8])

    settle(reduced)
    q0 = chip_sum(0)
    halves = []
    for h in range(2):
        zmsg[1, h].wait_recv()
        zmsg[-1, h].wait_recv()
        halves.append(
            q0[:, h * HALF : (h + 1) * HALF]
            + (zp_ref[3, h].astype(f32) + zm_ref[3, h].astype(f32)))
    grs = unproject(jnp.concatenate(halves, axis=1), raws_ref, inv_s)
    smsg = head_exchange(0, grs)
    lr_ref[4] = gather_loss(0, NX, x, lmsg)
    lmsg = [send(lr_ref.at[4], lr_ref.at[4 + NY - d], dev(dy=d)) for d in range(1, NY)]

    for copy in p2a + p2b:
        copy.wait_recv()
    for d in range(NX - 1):
        gh0 = gh0 + p2h0_ref[d].astype(f32)
        gh1 = gh1 + p2h1_ref[d].astype(f32)
    gro = unproject(jnp.concatenate([gh0.T, gh1.T], axis=1), rawo_ref, inv_o)
    omsg = head_exchange(1, gro)
    smsg = head_first(0, smsg)
    omsg = head_first(1, omsg)
    gsar_ref[...] = dot_nt(grs, ws_ref[...]).astype(bf16)
    gopt_ref[...] = dot_nt(gro, wo_ref[...]).astype(bf16)
    lr_ref[8] = gather_loss(4, NY, y, lmsg)
    lmsg = [send(lr_ref.at[8], lr_ref.at[8 + NZ - d], dev(dz=d)) for d in range(1, NZ)]
    heads = len(sent)
    smsg = head_second(0, smsg)
    omsg = head_second(1, omsg)
    lr_ref[16] = gather_loss(8, NZ, z, lmsg)
    lmsg = [send(lr_ref.at[16], lr_ref.at[17], dev(dc=1))]
    smsg = head_third(0, smsg)
    omsg = head_third(1, omsg)
    loss_ref[0] = jnp.sum(gather_loss(16, 2, c, lmsg)) * (1.0 / (2.0 * NX * NY * NZ * 2 * R))
    settle(heads)
    smsg = head_fourth(0, smsg)
    omsg = head_fourth(1, omsg)
    head_out(0, smsg, gws_ref)
    head_out(1, omsg, gwo_ref)

    settle(len(sent))


def local(sar_feats, opt_feats, w_sar, w_opt, logit_scale, partner):
    V = pltpu.VMEM
    scratch = [
        V((TR, E), bf16), V((E, TR), bf16), V((TC, E), bf16),
        V((NX, TR, E), f32), V((TR, TC), bf16), V((R, E), f32), V((R, E), f32),
        V((2, NZ, 8, R), f32), V((TR, R), f32), V((8, TC), f32),
        V((2, TR, R), f32), V((2, 8, TC), f32), V((TR, R), f32),
        V((16, R), f32), V((16, R), f32), V((NZ - 1, 16, R), f32), V((15, 16, R), f32),
        V((2, 16, R), f32), V((16, R), f32), V((16, R), f32), V((2, 16, R), f32),
        V((8, TC), f32), V((TR, R), f32), V((NX, E, E), bf16), V((3, HALF, E), bf16), V((3, NX, HALF, R), bf16),
        V((HALF, E), bf16), V((NX, HALF, R), bf16), V((3, HALF, R), bf16), V((3, HALF, R), bf16),
        V((NZ, R, E), f32), V((NZ, R, E), bf16), V((NZ, R, E), bf16), V((NZ, 2, R, HALF), bf16),
        V((4, 2, R, HALF), bf16), V((4, 2, R, HALF), bf16),
        V((2, R, F), bf16), V((2, F, 2 * R), bf16),
        V((2, R, HALF), bf16), V((2, R, HALF), bf16), V((2, R, HALF), bf16),
        V((2, NX, HALF, R), bf16), V((2, NY, HALF, R), bf16),
        V((2, 3, HALF, R), bf16), V((2, 3, HALF, R), bf16),
        V((2, NY, 64, R), bf16), V((2, NX, 64, R), bf16),
        V((2, 3, 64, R), bf16), V((2, 3, 64, R), bf16),
        V((2, NZ, 8, HALF), f32), V((2, NZ - 1, 8, HALF), f32),
        V((2, 8, HALF), f32), V((2, 8, HALF), f32),
        V((18, 8, R), f32),
        V((R, F), bf16), V((R, F), bf16), V((F, E), bf16), V((F, E), bf16),
        pltpu.SemaphoreType.DMA((MSGS,)), pltpu.SemaphoreType.DMA((MSGS,)),
        pltpu.SemaphoreType.DMA((4,)),
    ]
    vm = pl.BlockSpec(memory_space=pltpu.VMEM)
    hb = pl.BlockSpec(memory_space=pl.ANY)
    sm = pl.BlockSpec(memory_space=pltpu.SMEM)
    shapes = (
        jax.ShapeDtypeStruct((1,), f32),
        jax.ShapeDtypeStruct((R, F), bf16),
        jax.ShapeDtypeStruct((R, F), bf16),
        jax.ShapeDtypeStruct((4, E), f32),
        jax.ShapeDtypeStruct((4, E), f32),
    )
    outs = pl.pallas_call(
        kernel,
        out_shape=shapes,
        in_specs=[hb, hb, hb, hb, sm, vm],
        out_specs=(sm, vm, vm, vm, vm),
        scratch_shapes=scratch,
        compiler_params=pltpu.CompilerParams(
            collective_id=0, has_side_effects=True, vmem_limit_bytes=62 * 1024 * 1024),
        name="contrastive",
    )(sar_feats, opt_feats, w_sar, w_opt, logit_scale, partner.reshape(NY * 2, R))
    return pl.pallas_call(
        hand_over,
        out_shape=shapes,
        in_specs=[sm, vm, vm, vm, vm],
        out_specs=(sm, vm, vm, vm, vm),
        name="hand_over",
    )(*outs)


def hand_over(l_in, a_in, b_in, c_in, d_in, l_out, a_out, b_out, c_out, d_out):
    l_out[0] = l_in[0]
    for i, o in ((a_in, a_out), (b_in, b_out), (c_in, c_out), (d_in, d_out)):
        o[...] = i[...]


def solution(mesh):
    return jax.shard_map(
        local,
        mesh=mesh,
        in_specs=(
            P(("wide", "narrow"), None),
            P(("wide", "narrow"), None),
            P(),
            P(),
            P(),
            P("wide"),
        ),
        out_specs=(
            P(),
            P(("wide", "narrow"), None),
            P(("wide", "narrow"), None),
            P(("wide", "narrow"), None),
            P(("wide", "narrow"), None),
        ),
        check_vma=False,
    )
```
